32 devices in a mesh: dp: 2 (over y), rot: 16 (over z, x, core).
Axes of the slice: x: 2, y: 2, z: 4, core: 2. Of those that a mesh axis runs over, the one named last changes fastest.
Arguments:
- frames: int32 [32, 128, 512], P('dp'), may hold values from 0 to 8, as said below
- slices: float32 [32, 128, 512], P('rot'), may hold values from 0.125 to 8, as said below
Outputs:
- log_resp: float32 [32, 32, 512], P('dp', 'rot')
- new_slices: float32 [32, 128, 512], P('rot', 'dp')
The draws below stay inside these ranges and needn't reach their ends.
Inputs may be any that keep to these rules, and one draw needn't show every extreme that they name: `frames`: photon counts; each frame has its own brightness level. `slices`: positive intensities.
All inputs are finite; a program needn't handle non-finite values.
Results may differ from the reference program's by a relative error of at most 0.0012.
Values sent between devices are 32-bit elements; how exact they have to be, the bound alone decides.
No kernel may reach another device: no remote copies, remote signals or barrier semaphores. Data moves between devices by JAX's collectives and lax.ppermute only.
A program may use at most 64 MiB of HBM per device.

```python
import math
import jax
import jax.numpy as jnp
from jax import lax

R = 128
PHI = 512
FRAMES = 32
TILTS = 32


def draw_frames(key, part):
    first, second = jax.random.split(jax.random.fold_in(key, 11))
    levels = jax.random.randint(first, (FRAMES, 1, 1), 1, 9)
    levels = jnp.where(jnp.arange(FRAMES)[:, None, None] == 0, 8, levels)
    raw = jax.random.randint(second, (FRAMES, R, PHI), 0, 1 << 20)
    return (raw % (levels + 1)).astype(jnp.int32)


def draw_slices(key, part):
    first = jax.random.fold_in(jax.random.fold_in(key, 23), 0)
    base = jnp.exp(jax.random.uniform(first, (TILTS, R, PHI), jnp.float32, -jnp.log(2.0), jnp.log(2.0)))
    return base.astype(jnp.float32)


def setup_inputs(seed: int = 0) -> dict:
    key_list = jax.random.split(jax.random.key(seed), 3)
    frames = draw_frames(jax.random.fold_in(key_list[2], 71), 0)
    slices = draw_slices(jax.random.fold_in(key_list[2], 71), 0)
    return dict(frames=frames, slices=slices)


HIGH = lax.Precision.HIGHEST

def angle_tables(length):
    index = jnp.arange(length, dtype=jnp.int32)
    phase = index[:, None] * index[None, :] % length
    radians = phase.astype(jnp.float32) * (2.0 * math.pi / length)
    return (jnp.cos(radians), jnp.sin(radians))

def spectral_cross_terms(left_re, left_im, right_re, right_im, form):
    real_part = jnp.einsum(form, left_re, right_re, precision=HIGH) + jnp.einsum(form, left_im, right_im, precision=HIGH)
    imag_part = jnp.einsum(form, left_im, right_re, precision=HIGH) - jnp.einsum(form, left_re, right_im, precision=HIGH)
    return jnp.concatenate([real_part, imag_part], axis=-1)

def reference(frames, slices):
    frame_count, shells, angles = frames.shape
    tilt_count = slices.shape[0]
    cosine, sine = angle_tables(angles)
    forward = jnp.concatenate([cosine, -sine], axis=1)
    inverse = jnp.concatenate([cosine, -sine], axis=0) / angles
    counts = frames.astype(jnp.bfloat16)
    frame_spec = jnp.dot(counts.reshape(-1, angles), forward.astype(jnp.bfloat16), preferred_element_type=jnp.float32)
    frame_spec = frame_spec.reshape(frame_count, shells, 2 * angles)
    model_spec = jnp.dot(jnp.log(slices).reshape(-1, angles), forward, precision=HIGH)
    model_spec = model_spec.reshape(tilt_count, shells, 2 * angles)
    frame_real, frame_imaginary = (frame_spec[..., :angles], frame_spec[..., angles:])
    model_real, model_imaginary = (model_spec[..., :angles], model_spec[..., angles:])
    cross_product = spectral_cross_terms(frame_real, frame_imaginary, model_real, model_imaginary, 'wlg,ilg->wig')
    corr = jnp.dot(cross_product.reshape(-1, 2 * angles), inverse, precision=HIGH).reshape(frame_count, tilt_count, angles)
    totals = lax.optimization_barrier(jnp.sum(slices, axis=(1, 2)))
    anneal = 4.0 / math.sqrt(shells * angles)
    scores = anneal * (corr - totals[None, :, None])
    top = lax.optimization_barrier(jnp.max(scores, axis=(1, 2)))
    lse = top + jnp.log(lax.optimization_barrier(jnp.sum(jnp.exp(scores - top[:, None, None]), axis=(1, 2))))
    log_resp = scores - lse[:, None, None]
    resp = jnp.exp(log_resp)
    resp_spec = jnp.dot(resp.reshape(-1, angles), forward, precision=HIGH).reshape(frame_count, tilt_count, 2 * angles)
    responsibility_real, responsibility_imaginary = (resp_spec[..., :angles], resp_spec[..., angles:])
    back_projection = spectral_cross_terms(frame_real, frame_imaginary, responsibility_real, responsibility_imaginary, 'sha,sxa->xha')
    numer = jnp.dot(back_projection.reshape(-1, 2 * angles), inverse, precision=HIGH).reshape(tilt_count, shells, angles)
    weight = lax.optimization_barrier(jnp.sum(resp, axis=(0, 2)))
    new_slices = (numer + slices) / (weight[:, None, None] + 1.0)
    return (log_resp, new_slices)
```

```python
import functools
import math

import jax
import jax.numpy as jnp
import ml_dtypes
import numpy as np
from jax import lax
from jax.experimental import pallas as pl
from jax.experimental.pallas import tpu as pltpu
from jax.sharding import PartitionSpec as P

BF = jnp.bfloat16
F32 = jnp.float32
LANES = 128
SUB = 8
VMEM_BYTES = 24 * 1024 * 1024


def spectrum_tables(n):
    half, quarter = n // 2, n // 4
    index = np.arange(half)
    pieces = []
    for odd in (0, 1):
        theta = (np.outer(index, 2 * np.arange(quarter) + odd) % n) * (2.0 * np.pi / n)
        table = np.concatenate([np.cos(theta), -np.sin(theta)], axis=1)
        if not odd:
            table[:, quarter] = np.where(index % 2 == 0, 1.0, -1.0)
        table = table.astype(np.float32)
        head = table.astype(ml_dtypes.bfloat16)
        pieces += [head, (table - head.astype(np.float32)).astype(ml_dtypes.bfloat16)]
    return np.stack(pieces)


def split2(x):
    head = x.astype(BF)
    return head, (x - head.astype(F32)).astype(BF)


def mm(a, b):
    return jnp.dot(a, b, preferred_element_type=F32)


def mm_t(a, b):
    return lax.dot_general(a, b, (((1,), (1,)), ((), ())), preferred_element_type=F32)


def times_table(x, table, odd, product=mm):
    rows = x.shape[0]
    x0, x1 = split2(x)
    both = product(jnp.concatenate([x0, x1], axis=0), table[2 * odd])
    return both[:rows] + (both[rows:] + product(x0, table[2 * odd + 1]))


def fold(x):
    half = x.shape[-1] // 2
    low, high = x[..., :half], x[..., half:]
    return low + high, low - high


def to_half_spectrum(x, table):
    return [times_table(part, table, odd) for odd, part in enumerate(fold(x))]


def from_half_spectrum(even, odd, table):
    n = 2 * even.shape[1]
    lane = lax.broadcasted_iota(jnp.int32, even.shape, 1)
    weight = jnp.where((lane == 0) | (lane == n // 4), 1.0 / n, 2.0 / n)
    even = times_table(even * weight, table, 0, mm_t)
    odd = times_table(odd * (2.0 / n), table, 1, mm_t)
    return jnp.concatenate([even + odd, even - odd], axis=1)


def sublane_sums(parts):
    row = lax.broadcasted_iota(jnp.int32, parts[0].shape, 0)
    width = SUB // 2
    while width:
        low = (row & width) == 0
        merged = []
        for i in range(width):
            a, b = parts[i], parts[i + width]
            kept, moved = jnp.where(low, a, b), jnp.where(low, b, a)
            if 2 * width == SUB:
                moved = pltpu.roll(moved, width, 0)
            else:
                moved = jnp.where(low, pltpu.roll(moved, SUB - width, 0), pltpu.roll(moved, width, 0))
            merged.append(kept + moved)
        parts = merged
        width //= 2
    return parts[0]


def lane_zero(shape):
    return lax.broadcasted_iota(jnp.int32, shape, len(shape) - 1) == 0


def even_forms(re, im):
    first = lane_zero(re.shape)
    return re, jnp.where(first, 0.0, im), jnp.where(first, im, re)


def expect_kernel(anneal, chunk, groups, mine, frames, slices, table, *refs):
    count, shells, angles = frames.shape
    tilts = slices.shape[0]
    half = angles // 2
    quarter = angles // 4
    chunks = count // chunk
    share = shells // groups
    rows = tilts * shells
    other, refs = refs[: groups - 1], refs[groups - 1 :]
    own_out, scores, local, own, fbuf, sbuf, tv, ya, yb, yc, cross, sems = refs
    spec = (own, *other)
    bases = [pl.multiple_of(lax.rem(mine[0] + s, groups) * share, SUB) for s in range(groups)]

    def frame_copy(c):
        at = pl.ds(c * chunk, chunk)
        return pltpu.make_async_copy(frames.at[at], fbuf.at[at], sems.at[2 + c])

    def own_copy(c):
        at = pl.ds(c * chunk, chunk)
        return pltpu.make_async_copy(own.at[at], own_out.at[at], sems.at[2 + chunks + c])

    table_copy = pltpu.make_async_copy(table, tv, sems.at[0])
    slice_copy = pltpu.make_async_copy(slices, sbuf, sems.at[1])
    table_copy.start()
    slice_copy.start()
    for c in range(chunks):
        frame_copy(c).start()

    table_copy.wait()
    slice_copy.wait()
    logs = jnp.log(sbuf[...]).reshape(rows, angles)
    even, odd = to_half_spectrum(logs, tv)
    a, b, c = even_forms(even[:, :quarter], even[:, quarter:])
    ya[:, :quarter] = jnp.where(lane_zero(a.shape), jnp.sum(logs, axis=1, keepdims=True), a)
    yb[:, :quarter] = b
    yc[...] = c
    ya[:, quarter:] = odd[:, :quarter]
    yb[:, quarter:] = odd[:, quarter:]

    def transform(c):
        at = pl.ds(c * chunk, chunk)
        folded = [fold(fbuf[at, pl.ds(base, share), :]) for base in bases]
        for odd in range(2):
            counts = [part[odd].astype(F32).astype(BF).reshape(chunk * share, half) for part in folded]
            result = mm(jnp.concatenate(counts, axis=0), tv[2 * odd])
            for s in range(groups):
                spec[s][at, :, odd * half : (odd + 1) * half] = result[
                    s * chunk * share : (s + 1) * chunk * share
                ].reshape(chunk, share, half)

    def correlate(c):
        out = pl.ds(c * SUB, SUB)
        for odd in range(2):
            for lanes in range(0, quarter, LANES):
                re_l = pl.ds(odd * half + lanes, LANES)
                im_l = pl.ds(odd * half + quarter + lanes, LANES)
                y_l = pl.ds(odd * quarter + lanes, LANES)
                re, im = [None] * SUB, [None] * SUB
                for pair in range(0, chunk, 2):
                    for s in range(groups):
                        for g in range(share // SUB):
                            r = pl.ds(g * SUB, SUB)
                            ks = [c * chunk + pair + q for q in range(2)]
                            xs = [(spec[s][k, r, re_l], spec[s][k, r, im_l]) for k in ks]
                            for t in range(tilts):
                                y = pl.ds(bases[s] + (t * shells + g * SUB), SUB)
                                a, b = ya[y, y_l], yb[y, y_l]
                                c_ = a if odd else yc[y, pl.ds(lanes, LANES)]
                                for q in range(2):
                                    xr, xi = xs[q]
                                    u = xr * a + xi * b
                                    v = xi * c_ - xr * b
                                    at = t * chunk + pair + q
                                    re[at] = u if re[at] is None else re[at] + u
                                    im[at] = v if im[at] is None else im[at] + v
                cross[out, re_l] = sublane_sums(re)
                cross[out, im_l] = sublane_sums(im)

    frame_copy(0).wait()
    transform(0)
    for c in range(1, chunks):
        frame_copy(c).wait()
        correlate(c - 1)
        transform(c)
        own_copy(c - 1).start()
    own_copy(chunks - 1).start()
    correlate(chunks - 1)

    spectrum = cross[...]
    dc = spectrum[:, :1]
    even = spectrum[:, :half]
    even = jnp.where(lane_zero(even.shape), 0.0, even)
    corr = from_half_spectrum(even, spectrum[:, half:], tv) + dc * (1.0 / angles)
    totals = [
        jnp.broadcast_to(jnp.sum(jnp.sum(sbuf[t], axis=0, keepdims=True), axis=1, keepdims=True), (chunk, 1))
        for t in range(tilts)
    ]
    part = anneal * (corr - jnp.concatenate(totals * chunks, axis=0))
    scores[...] = part

    def over_tilts(x, join):
        parts = []
        for c in range(chunks):
            group = x[c * SUB : (c + 1) * SUB]
            shift = chunk
            while shift < SUB:
                group = join(group, pltpu.roll(group, shift, 0))
                shift *= 2
            parts.append(group)
        return jnp.concatenate(parts, axis=0)

    wide = local.shape
    top = over_tilts(jnp.broadcast_to(jnp.max(part, axis=1, keepdims=True), wide), jnp.maximum)
    total = jnp.sum(jnp.exp(part - top[:, :1]), axis=1, keepdims=True)
    local[...] = top + jnp.log(over_tilts(jnp.broadcast_to(total, wide), jnp.add))
    for c in range(chunks):
        own_copy(c).wait()


def in_hbm(x):
    return pltpu.with_memory_space_constraint(x, pltpu.HBM)


def expect(frames, slices, table, anneal, mine, groups):
    count, shells, angles = frames.shape
    tilts = slices.shape[0]
    half = angles // 2
    chunk = SUB // tilts
    share = shells // groups
    hbm = pl.BlockSpec(memory_space=pltpu.HBM)
    vm = pl.BlockSpec(memory_space=pltpu.VMEM)
    form = pltpu.VMEM((tilts * shells, half), F32)
    *other, own, scores, local = pl.pallas_call(
        functools.partial(expect_kernel, anneal, chunk, groups),
        out_shape=(
            *[pltpu.VMEM((count, share, angles), F32)] * (groups - 1),
            pltpu.HBM((count, share, angles), F32),
            pltpu.VMEM((tilts * count, angles), F32),
            pltpu.VMEM((tilts * count, LANES), F32),
        ),
        in_specs=[pl.BlockSpec(memory_space=pltpu.SMEM)] + [hbm] * 3,
        out_specs=(*[vm] * (groups - 1), hbm, vm, vm),
        scratch_shapes=[
            pltpu.VMEM((count, share, angles), F32),
            pltpu.VMEM((count, shells, angles), jnp.int32),
            pltpu.VMEM((tilts, shells, angles), F32),
            pltpu.VMEM(table.shape, BF),
            form,
            form,
            pltpu.VMEM((tilts * shells, half // 2), F32),
            pltpu.VMEM((tilts * count, angles), F32),
            pltpu.SemaphoreType.DMA((2 + 2 * (count // chunk),)),
        ],
        compiler_params=pltpu.CompilerParams(vmem_limit_bytes=VMEM_BYTES),
        name="expect",
    )(mine[None], *(in_hbm(x) for x in (frames, slices, table)))
    return (own, *other), scores, local


def weights_kernel(scores, local, table, out):
    own = jnp.exp(scores[...] - local[:, :1])
    out[...] = jnp.concatenate(to_half_spectrum(own, table), axis=1)


def row_of(k, t, tilts):
    chunk = SUB // tilts
    return k // chunk * SUB + t * chunk + k % chunk


def back_kernel(spec, transformed, local, lse, out, fa, fb, fc):
    count, share, angles = spec.shape
    half, quarter = angles // 2, angles // 4
    sections = angles // LANES
    tilts = transformed.shape[0] // count
    rows = tilts * share
    scaled = transformed[...] * jnp.exp(local[:, :1] - lse[:, :1])
    a, b, c = even_forms(scaled[:, :quarter], scaled[:, quarter:half])
    fa[:, :quarter] = a
    fb[:, :quarter] = b
    fc[...] = c
    fa[:, quarter:] = scaled[:, half : half + quarter]
    fb[:, quarter:] = scaled[:, half + quarter :]
    for odd in range(2):
        for lanes in range(0, quarter, LANES):
            re_l = pl.ds(odd * half + lanes, LANES)
            im_l = pl.ds(odd * half + quarter + lanes, LANES)
            p_l = pl.ds(odd * quarter + lanes, LANES)
            for g in range(share // SUB):
                r = pl.ds(g * SUB, SUB)
                re, im = [None] * tilts, [None] * tilts
                for k in range(count):
                    xr, xi = spec[k, r, re_l], spec[k, r, im_l]
                    for t in range(tilts):
                        row = pl.ds(row_of(k, t, tilts), 1)
                        a, b = fa[row, p_l], fb[row, p_l]
                        c = a if odd else fc[row, pl.ds(lanes, LANES)]
                        u = xr * a + xi * b
                        v = xi * c - xr * b
                        re[t] = u if k == 0 else re[t] + u
                        im[t] = v if k == 0 else im[t] + v
                for t in range(tilts):
                    at = t * share + g * SUB
                    out[pl.ds((odd * half + lanes) // LANES * rows + at, SUB), :] = re[t]
                    out[pl.ds((odd * half + quarter + lanes) // LANES * rows + at, SUB), :] = im[t]
    tilt_of = lax.broadcasted_iota(jnp.int32, (tilts * count, 1), 0) % SUB // (SUB // tilts)
    sums = [jnp.sum(jnp.where(tilt_of == t, scaled[:, :1], 0.0), axis=0, keepdims=True) for t in range(tilts)]
    tail = jnp.concatenate(sums + [jnp.zeros((out.shape[0] - sections * rows - tilts, 1), F32)], axis=0)
    out[pl.ds(sections * rows, tail.shape[0]), :] = jnp.broadcast_to(tail, (tail.shape[0], LANES))


def back(spec, transformed, local, lse):
    count, share, angles = spec.shape
    half = angles // 2
    tilts = transformed.shape[0] // count
    rows = tilts * share * (angles // LANES) + -(-tilts // SUB) * SUB
    vm = pl.BlockSpec(memory_space=pltpu.VMEM)
    form = pltpu.VMEM((tilts * count, half), F32)
    return pl.pallas_call(
        back_kernel,
        out_shape=pltpu.VMEM((rows, LANES), F32),
        in_specs=[vm] * 4,
        out_specs=vm,
        scratch_shapes=[form, form, pltpu.VMEM((tilts * count, half // 2), F32)],
        compiler_params=pltpu.CompilerParams(vmem_limit_bytes=VMEM_BYTES),
        cost_estimate=pl.CostEstimate(flops=8 * count * tilts * share * half, bytes_accessed=count * share * angles * 4, transcendentals=0),
        name="back",
    )(spec, transformed, local, lse)


def log_kernel(scores, lse, out):
    count, tilts, _ = out.shape
    chunk = SUB // tilts
    value = scores[...] - lse[:, :1]
    for c in range(count // chunk):
        for t in range(tilts):
            at = c * SUB + t * chunk
            out[pl.ds(c * chunk, chunk), t, :] = value[at : at + chunk]


def update_kernel(mine, own, other, slices, table, out):
    tilts, share, angles = out.shape
    half = angles // 2
    sections = angles // LANES
    rows = tilts * share

    def columns(first, last):
        at = [pl.ds(s * rows, rows) for s in range(first, last)]
        return jnp.concatenate([own[r, :] + other[r, :] for r in at], axis=1)

    numer = from_half_spectrum(columns(0, sections // 2), columns(sections // 2, sections), table)
    base = pl.multiple_of(mine[0] * share, SUB)
    for t in range(tilts):
        at = pl.ds(sections * rows + t, 1)
        weight = own[at, :1] + other[at, :1]
        out[t] = (numer[t * share : (t + 1) * share] + slices[t, pl.ds(base, share), :]) / (weight + 1.0)


def log_sum(a, b):
    return jnp.maximum(a, b) + jnp.log(1.0 + jnp.exp(-jnp.abs(a - b)))


def over_axis(value, axis):
    size = lax.axis_size(axis)
    if size & (size - 1):
        return jax.nn.logsumexp(lax.all_gather(value, axis), axis=0)
    bit = 1
    while bit < size:
        step = bit | 1
        value = log_sum(value, lax.ppermute(value, axis, [(i, i ^ step) for i in range(size)]))
        bit *= 2
    return value


def on_device(frames, slices):
    count, shells, angles = frames.shape
    tilts = slices.shape[0]
    anneal = 4.0 / math.sqrt(shells * angles)
    groups = lax.axis_size("dp")
    mine = lax.axis_index("dp").astype(jnp.int32)
    share = shells // groups
    table = jnp.asarray(spectrum_tables(angles))
    vm = pl.BlockSpec(memory_space=pltpu.VMEM)
    params = pltpu.CompilerParams(vmem_limit_bytes=VMEM_BYTES)

    spec, scores, local = expect(frames, slices, table, anneal, mine, groups)
    transformed = pl.pallas_call(
        weights_kernel,
        out_shape=pltpu.VMEM((tilts * count, angles), F32),
        in_specs=[vm] * 3,
        out_specs=vm,
        compiler_params=params,
        cost_estimate=pl.CostEstimate(flops=3 * tilts * count * angles * angles, bytes_accessed=2 * angles * angles, transcendentals=0),
        name="transform",
    )(scores, local, table)
    lse = over_axis(local, "rot")

    others = None
    for step in range(1, groups):
        block = back(spec[step], transformed, local, lse)
        got = lax.ppermute(block, "dp", [(i, (i + step) % groups) for i in range(groups)])
        others = got if others is None else others + got
    own = back(spec[0], transformed, local, lse)
    if others is None:
        others = jnp.zeros_like(own)
    log_resp = pl.pallas_call(
        log_kernel,
        out_shape=jax.ShapeDtypeStruct((count, tilts, angles), F32),
        in_specs=[vm, vm],
        out_specs=vm,
        compiler_params=params,
        name="log_resp",
    )(scores, lse)
    new_slices = pl.pallas_call(
        update_kernel,
        out_shape=jax.ShapeDtypeStruct((tilts, share, angles), F32),
        in_specs=[pl.BlockSpec(memory_space=pltpu.SMEM)] + [vm] * 4,
        out_specs=vm,
        compiler_params=params,
        name="update",
    )(mine[None], own, others, slices, table)
    return (log_resp, new_slices)


def solution(mesh):
    in_specs = (P("dp", None, None), P("rot", None, None))
    out_specs = (P("dp", "rot", None), P("rot", "dp", None))
    return jax.shard_map(on_device, mesh=mesh, in_specs=in_specs, out_specs=out_specs, check_vma=False)
```

```python
import functools
import math

import jax
import jax.numpy as jnp
import ml_dtypes
import numpy as np
from jax import lax
from jax.experimental import pallas as pl
from jax.experimental.pallas import tpu as pltpu
from jax.sharding import PartitionSpec as P

BF = jnp.bfloat16
F32 = jnp.float32
LANES = 128
SUB = 8
VMEM_BYTES = 24 * 1024 * 1024


def spectrum_tables(n):
    half, quarter = n // 2, n // 4
    index = np.arange(half)
    pieces = []
    for odd in (0, 1):
        theta = (np.outer(index, 2 * np.arange(quarter) + odd) % n) * (2.0 * np.pi / n)
        table = np.concatenate([np.cos(theta), -np.sin(theta)], axis=1)
        if not odd:
            table[:, quarter] = np.where(index % 2 == 0, 1.0, -1.0)
        table = table.astype(np.float32)
        head = table.astype(ml_dtypes.bfloat16)
        pieces += [head, (table - head.astype(np.float32)).astype(ml_dtypes.bfloat16)]
    return np.stack(pieces)


def split2(x):
    head = x.astype(BF)
    return head, (x - head.astype(F32)).astype(BF)


def mm(a, b):
    return jnp.dot(a, b, preferred_element_type=F32)


def mm_t(a, b):
    return lax.dot_general(a, b, (((1,), (1,)), ((), ())), preferred_element_type=F32)


def times_table(x, table, odd, product=mm):
    rows = x.shape[0]
    x0, x1 = split2(x)
    both = product(jnp.concatenate([x0, x1], axis=0), table[2 * odd])
    return both[:rows] + (both[rows:] + product(x0, table[2 * odd + 1]))


def fold(x):
    half = x.shape[-1] // 2
    low, high = x[..., :half], x[..., half:]
    return low + high, low - high


def to_half_spectrum(x, table):
    return [times_table(part, table, odd) for odd, part in enumerate(fold(x))]


def from_half_spectrum(even, odd, table):
    n = 2 * even.shape[1]
    lane = lax.broadcasted_iota(jnp.int32, even.shape, 1)
    weight = jnp.where((lane == 0) | (lane == n // 4), 1.0 / n, 2.0 / n)
    even = times_table(even * weight, table, 0, mm_t)
    odd = times_table(odd * (2.0 / n), table, 1, mm_t)
    return jnp.concatenate([even + odd, even - odd], axis=1)


def sublane_sums(parts):
    row = lax.broadcasted_iota(jnp.int32, parts[0].shape, 0)
    width = SUB // 2
    while width:
        low = (row & width) == 0
        merged = []
        for i in range(width):
            a, b = parts[i], parts[i + width]
            kept, moved = jnp.where(low, a, b), jnp.where(low, b, a)
            if 2 * width == SUB:
                moved = pltpu.roll(moved, width, 0)
            else:
                moved = jnp.where(low, pltpu.roll(moved, SUB - width, 0), pltpu.roll(moved, width, 0))
            merged.append(kept + moved)
        parts = merged
        width //= 2
    return parts[0]


def pack_rows(x):
    groups = x.shape[0] // SUB
    lane = lax.broadcasted_iota(jnp.int32, (SUB, LANES), 1)
    packed = x[:SUB]
    for i in range(1, groups):
        packed = jnp.where(lane >= i * (LANES // groups), x[i * SUB : (i + 1) * SUB], packed)
    return packed


def unpack_rows(packed, groups):
    step = LANES // groups
    return jnp.concatenate([packed[:, i * step : i * step + 1] for i in range(groups)], axis=0)


def lane_zero(shape):
    return lax.broadcasted_iota(jnp.int32, shape, len(shape) - 1) == 0


def even_forms(re, im):
    first = lane_zero(re.shape)
    return re, jnp.where(first, 0.0, im), jnp.where(first, im, re)


def spectra(counts, table):
    shape = counts.shape[:2]
    half = counts.shape[2] // 2
    return [
        mm(part.reshape(-1, half), table[2 * odd]).reshape(*shape, half)
        for odd, part in enumerate(fold(counts.astype(F32).astype(BF)))
    ]


def own_shells(step, share):
    groups = lax.axis_size("dp")
    return pl.multiple_of(lax.rem(lax.axis_index("dp") + step, groups) * share, SUB)


def expect_kernel(anneal, chunk, groups, frames, slices, table, *refs):
    count, shells, angles = frames.shape
    tilts = slices.shape[0]
    half, quarter = angles // 2, angles // 4
    chunks = count // chunk
    share = shells // groups
    rows = tilts * shells
    other, refs = refs[: groups - 1], refs[groups - 1 :]
    scores, local, own, fbuf, sbuf, tv, ya, yb, yc, cross, sems = refs
    spec = (own, *other)
    bases = [own_shells(s, share) for s in range(groups)]

    def frame_copy(c):
        at = pl.ds(c * chunk, chunk)
        return pltpu.make_async_copy(frames.at[at], fbuf.at[at], sems.at[2 + c])

    table_copy = pltpu.make_async_copy(table, tv, sems.at[0])
    slice_copy = pltpu.make_async_copy(slices, sbuf, sems.at[1])

    def transform(c):
        at = pl.ds(c * chunk, chunk)
        counts = jnp.concatenate([fbuf[at, pl.ds(base, share), :] for base in bases], axis=1)
        for odd, part in enumerate(spectra(counts, tv)):
            for s in range(groups):
                spec[s][at, :, odd * half : (odd + 1) * half] = part[:, s * share : (s + 1) * share]

    def correlate(c):
        out = pl.ds(c * SUB, SUB)
        for odd in range(2):
            for lanes in range(0, quarter, LANES):
                re_l = pl.ds(odd * half + lanes, LANES)
                im_l = pl.ds(odd * half + quarter + lanes, LANES)
                y_l = pl.ds(odd * quarter + lanes, LANES)
                sums = [[None] * SUB for _ in range(3)]
                for pair in range(0, chunk, 2):
                    for s in range(groups):
                        for g in range(share // SUB):
                            r = pl.ds(g * SUB, SUB)
                            ks = [c * chunk + pair + q for q in range(2)]
                            xs = [(spec[s][k, r, re_l], spec[s][k, r, im_l]) for k in ks]
                            xs = [(xr, xi, xr + xi) for xr, xi in xs]
                            for t in range(tilts):
                                y = pl.ds(bases[s] + (t * shells + g * SUB), SUB)
                                ys = ya[y, y_l], yb[y, y_l], yc[y, y_l]
                                for q in range(2):
                                    at = t * chunk + pair + q
                                    for i in range(3):
                                        u = xs[q][i] * ys[i]
                                        sums[i][at] = u if sums[i][at] is None else sums[i][at] + u
                m = [sublane_sums(part) for part in sums]
                re, im = m[0] + m[1], m[2] - m[0] + m[1]
                if lanes == 0 and not odd:
                    first = lane_zero(re.shape)
                    re, im = jnp.where(first, m[0], re), jnp.where(first, m[1], im)
                cross[out, re_l] = re
                cross[out, im_l] = im

    slice_copy.start()
    table_copy.start()
    for c in range(chunks):
        frame_copy(c).start()

    slice_copy.wait()
    logs = jnp.log(sbuf[...]).reshape(rows, angles)
    folded = fold(logs)
    dc = jnp.sum(logs, axis=1, keepdims=True)
    table_copy.wait()
    even, odd = [times_table(part, tv, i) for i, part in enumerate(folded)]
    even_re = jnp.where(lane_zero((rows, quarter)), dc, even[:, :quarter])
    for i, (re, im) in enumerate(((even_re, even[:, quarter:]), (odd[:, :quarter], odd[:, quarter:]))):
        at = slice(i * quarter, (i + 1) * quarter)
        ya[:, at] = re
        yb[:, at] = im
        yc[:, at] = re - im

    frame_copy(0).wait()
    transform(0)
    for c in range(1, chunks):
        frame_copy(c).wait()
        transform(c)
        correlate(c - 1)
    correlate(chunks - 1)

    spectrum = cross[...]
    dc = spectrum[:, :1]
    even = spectrum[:, :half]
    even = jnp.where(lane_zero(even.shape), 0.0, even)
    corr = from_half_spectrum(even, spectrum[:, half:], tv) + dc * (1.0 / angles)
    totals = [
        jnp.broadcast_to(jnp.sum(jnp.sum(sbuf[t], axis=0, keepdims=True), axis=1, keepdims=True), (chunk, 1))
        for t in range(tilts)
    ]
    part = anneal * (corr - jnp.concatenate(totals * chunks, axis=0))
    scores[...] = part

    def over_tilts(x, join):
        parts = []
        for c in range(chunks):
            group = x[c * SUB : (c + 1) * SUB]
            shift = chunk
            while shift < SUB:
                group = join(group, pltpu.roll(group, shift, 0))
                shift *= 2
            parts.append(group)
        return jnp.concatenate(parts, axis=0)

    wide = (tilts * count, LANES)
    top = over_tilts(jnp.broadcast_to(jnp.max(part, axis=1, keepdims=True), wide), jnp.maximum)
    total = jnp.sum(jnp.exp(part - top[:, :1]), axis=1, keepdims=True)
    local[...] = pack_rows(top + jnp.log(over_tilts(jnp.broadcast_to(total, wide), jnp.add)))


def in_hbm(x):
    return pltpu.with_memory_space_constraint(x, pltpu.HBM)


def expect(frames, slices, table, anneal, groups):
    count, shells, angles = frames.shape
    tilts = slices.shape[0]
    half = angles // 2
    chunk = SUB // tilts
    share = shells // groups
    hbm = pl.BlockSpec(memory_space=pltpu.HBM)
    vm = pl.BlockSpec(memory_space=pltpu.VMEM)
    form = pltpu.VMEM((tilts * shells, half), F32)
    *other, scores, local = pl.pallas_call(
        functools.partial(expect_kernel, anneal, chunk, groups),
        out_shape=(
            *[pltpu.VMEM((count, share, angles), F32)] * (groups - 1),
            pltpu.VMEM((tilts * count, angles), F32),
            pltpu.VMEM((SUB, LANES), F32),
        ),
        in_specs=[hbm] * 3,
        out_specs=(*[vm] * (groups - 1), vm, vm),
        scratch_shapes=[
            pltpu.VMEM((count, share, angles), F32),
            pltpu.VMEM((count, shells, angles), jnp.int32),
            pltpu.VMEM((tilts, shells, angles), F32),
            pltpu.VMEM(table.shape, BF),
            form,
            form,
            form,
            pltpu.VMEM((tilts * count, angles), F32),
            pltpu.SemaphoreType.DMA((2 + count // chunk,)),
        ],
        compiler_params=pltpu.CompilerParams(vmem_limit_bytes=VMEM_BYTES),
        name="expect",
    )(*(in_hbm(x) for x in (frames, slices, table)))
    return other, scores, local


def weights_kernel(scores, local, table, out):
    own = jnp.exp(scores[...] - unpack_rows(local[...], scores.shape[0] // SUB))
    out[...] = jnp.concatenate(to_half_spectrum(own, table), axis=1)


def row_of(k, t, tilts):
    chunk = SUB // tilts
    return k // chunk * SUB + t * chunk + k % chunk


def back_project(spec, transformed, local, lse, out, fa, fb, fc):
    count, share, angles = spec.shape
    half, quarter = angles // 2, angles // 4
    sections = angles // LANES
    tilts = transformed.shape[0] // count
    rows = tilts * share
    scaled = transformed[...] * unpack_rows(jnp.exp(local[...] - lse[...]), tilts * count // SUB)
    for odd in range(2):
        re, im = scaled[:, odd * half : odd * half + quarter], scaled[:, odd * half + quarter : (odd + 1) * half]
        at = slice(odd * quarter, (odd + 1) * quarter)
        fa[:, at] = re
        fb[:, at] = im
        fc[:, at] = re - im
    for odd in range(2):
        for lanes in range(0, quarter, LANES):
            re_l = pl.ds(odd * half + lanes, LANES)
            im_l = pl.ds(odd * half + quarter + lanes, LANES)
            p_l = pl.ds(odd * quarter + lanes, LANES)
            for g in range(share // SUB):
                r = pl.ds(g * SUB, SUB)
                sums = [[None] * tilts for _ in range(3)]
                for k in range(count):
                    xr, xi = spec[k, r, re_l], spec[k, r, im_l]
                    xs = xr, xi, xr + xi
                    for t in range(tilts):
                        row = pl.ds(row_of(k, t, tilts), 1)
                        for i, form in enumerate((fa, fb, fc)):
                            u = xs[i] * form[row, p_l]
                            sums[i][t] = u if k == 0 else sums[i][t] + u
                for t in range(tilts):
                    m = [part[t] for part in sums]
                    re, im = m[0] + m[1], m[2] - m[0] + m[1]
                    if lanes == 0 and not odd:
                        first = lane_zero(re.shape)
                        re, im = jnp.where(first, m[0], re), jnp.where(first, m[1], im)
                    at = t * share + g * SUB
                    out[pl.ds((odd * half + lanes) // LANES * rows + at, SUB), :] = re
                    out[pl.ds((odd * half + quarter + lanes) // LANES * rows + at, SUB), :] = im
    tilt_of = lax.broadcasted_iota(jnp.int32, (tilts * count, 1), 0) % SUB // (SUB // tilts)
    sums = [jnp.sum(jnp.where(tilt_of == t, scaled[:, :1], 0.0), axis=0, keepdims=True) for t in range(tilts)]
    tail = jnp.concatenate(sums + [jnp.zeros((out.shape[0] - sections * rows - tilts, 1), F32)], axis=0)
    out[pl.ds(sections * rows, tail.shape[0]), :] = jnp.broadcast_to(tail, (tail.shape[0], LANES))


def back_own_kernel(transformed, local, lse, frames, table, out, counts, spec, fa, fb, fc, sem):
    count, share, angles = spec.shape
    half = angles // 2
    copy = pltpu.make_async_copy(frames.at[:, pl.ds(own_shells(0, share), share), :], counts, sem)
    copy.start()
    copy.wait()
    chunk = min(count, 8)

    def step(c, carry):
        at = pl.ds(c * chunk, chunk)
        for odd, part in enumerate(spectra(counts[at], table)):
            spec[at, :, odd * half : (odd + 1) * half] = part
        return carry

    lax.fori_loop(0, count // chunk, step, 0)
    back_project(spec, transformed, local, lse, out, fa, fb, fc)


def back(shape, transformed, local, lse, spec=None, frames=None, table=None):
    count, share, angles = shape
    half = angles // 2
    tilts = transformed.shape[0] // count
    rows = tilts * share * (angles // LANES) + -(-tilts // SUB) * SUB
    vm = pl.BlockSpec(memory_space=pltpu.VMEM)
    forms = [pltpu.VMEM((tilts * count, half), F32)] * 3
    call = functools.partial(
        pl.pallas_call,
        out_shape=pltpu.VMEM((rows, LANES), F32),
        out_specs=vm,
        compiler_params=pltpu.CompilerParams(vmem_limit_bytes=VMEM_BYTES),
        cost_estimate=pl.CostEstimate(flops=8 * count * tilts * share * half, bytes_accessed=count * share * angles * 4, transcendentals=0),
    )
    if spec is not None:
        return call(back_project, in_specs=[vm] * 4, scratch_shapes=forms, name="back")(spec, transformed, local, lse)
    return call(
        back_own_kernel,
        in_specs=[vm] * 3 + [pl.BlockSpec(memory_space=pltpu.HBM), vm],
        scratch_shapes=[
            pltpu.VMEM(shape, jnp.int32),
            pltpu.VMEM(shape, F32),
            *forms,
            pltpu.SemaphoreType.DMA,
        ],
        name="back_own",
    )(transformed, local, lse, in_hbm(frames), table)


def log_kernel(scores, lse, out):
    count, tilts, _ = out.shape
    chunk = SUB // tilts
    value = scores[...] - unpack_rows(lse[...], scores.shape[0] // SUB)
    for c in range(count // chunk):
        for t in range(tilts):
            at = c * SUB + t * chunk
            out[pl.ds(c * chunk, chunk), t, :] = value[at : at + chunk]


def update_kernel(own, other, slices, table, out):
    tilts, share, angles = out.shape
    half = angles // 2
    sections = angles // LANES
    rows = tilts * share

    def columns(first, last):
        at = [pl.ds(s * rows, rows) for s in range(first, last)]
        return jnp.concatenate([own[r, :] + other[r, :] for r in at], axis=1)

    numer = from_half_spectrum(columns(0, sections // 2), columns(sections // 2, sections), table)
    base = own_shells(0, share)
    for t in range(tilts):
        at = pl.ds(sections * rows + t, 1)
        weight = own[at, :1] + other[at, :1]
        out[t] = (numer[t * share : (t + 1) * share] + slices[t, pl.ds(base, share), :]) / (weight + 1.0)


def log_sum(a, b):
    return jnp.maximum(a, b) + jnp.log(1.0 + jnp.exp(-jnp.abs(a - b)))


def over_axis(value, axis):
    size = lax.axis_size(axis)
    if size & (size - 1):
        return jax.nn.logsumexp(lax.all_gather(value, axis), axis=0)
    bit = 1
    while bit < size:
        step = bit | 1
        value = log_sum(value, lax.ppermute(value, axis, [(i, i ^ step) for i in range(size)]))
        bit *= 2
    return value


def on_device(frames, slices):
    count, shells, angles = frames.shape
    tilts = slices.shape[0]
    anneal = 4.0 / math.sqrt(shells * angles)
    groups = lax.axis_size("dp")
    share = shells // groups
    table = jnp.asarray(spectrum_tables(angles))
    vm = pl.BlockSpec(memory_space=pltpu.VMEM)
    params = pltpu.CompilerParams(vmem_limit_bytes=VMEM_BYTES)

    spec, scores, local = expect(frames, slices, table, anneal, groups)
    transformed = pl.pallas_call(
        weights_kernel,
        out_shape=pltpu.VMEM((tilts * count, angles), F32),
        in_specs=[vm] * 3,
        out_specs=vm,
        compiler_params=params,
        cost_estimate=pl.CostEstimate(flops=3 * tilts * count * angles * angles, bytes_accessed=2 * angles * angles, transcendentals=0),
        name="transform",
    )(scores, local, table)
    lse = over_axis(local, "rot")

    shape = (count, share, angles)
    others = None
    for step in range(1, groups):
        block = back(shape, transformed, local, lse, spec=spec[step - 1])
        got = lax.ppermute(block, "dp", [(i, (i + step) % groups) for i in range(groups)])
        others = got if others is None else others + got
    own = back(shape, transformed, local, lse, frames=frames, table=table)
    if others is None:
        others = jnp.zeros_like(own)
    log_resp = pl.pallas_call(
        log_kernel,
        out_shape=jax.ShapeDtypeStruct((count, tilts, angles), F32),
        in_specs=[vm, vm],
        out_specs=vm,
        compiler_params=params,
        name="log_resp",
    )(scores, lse)
    new_slices = pl.pallas_call(
        update_kernel,
        out_shape=jax.ShapeDtypeStruct((tilts, share, angles), F32),
        in_specs=[vm] * 4,
        out_specs=vm,
        compiler_params=params,
        name="update",
    )(own, others, slices, table)
    return (log_resp, new_slices)


def solution(mesh):
    in_specs = (P("dp", None, None), P("rot", None, None))
    out_specs = (P("dp", "rot", None), P("rot", "dp", None))
    return jax.shard_map(on_device, mesh=mesh, in_specs=in_specs, out_specs=out_specs, check_vma=False)
```

```python
import functools
import math

import jax
import jax.numpy as jnp
import ml_dtypes
import numpy as np
from jax import lax
from jax.experimental import pallas as pl
from jax.experimental.pallas import tpu as pltpu
from jax.sharding import PartitionSpec as P

BF = jnp.bfloat16
F32 = jnp.float32
LANES = 128
SUB = 8
VMEM_BYTES = 24 * 1024 * 1024
VECTOR_COST = 128


def spectrum_tables(n):
    half, quarter = n // 2, n // 4
    index = np.arange(half)
    pieces = []
    for odd in (0, 1):
        theta = (np.outer(index, 2 * np.arange(quarter) + odd) % n) * (2.0 * np.pi / n)
        table = np.concatenate([np.cos(theta), -np.sin(theta)], axis=1)
        if not odd:
            table[:, quarter] = np.where(index % 2 == 0, 1.0, -1.0)
        table = table.astype(np.float32)
        head = table.astype(ml_dtypes.bfloat16)
        pieces += [head, (table - head.astype(np.float32)).astype(ml_dtypes.bfloat16)]
    return np.stack(pieces)


def split2(x):
    head = x.astype(BF)
    return head, (x - head.astype(F32)).astype(BF)


def mm(a, b):
    return jnp.dot(a, b, preferred_element_type=F32)


def mm_t(a, b):
    return lax.dot_general(a, b, (((1,), (1,)), ((), ())), preferred_element_type=F32)


def times_table(x, table, odd, product=mm):
    rows = x.shape[0]
    x0, x1 = split2(x)
    both = product(jnp.concatenate([x0, x1], axis=0), table[2 * odd])
    return both[:rows] + (both[rows:] + product(x0, table[2 * odd + 1]))


def fold(x):
    half = x.shape[-1] // 2
    low, high = x[..., :half], x[..., half:]
    return low + high, low - high


def to_half_spectrum(x, table):
    return [times_table(part, table, odd) for odd, part in enumerate(fold(x))]


def from_half_spectrum(even, odd, table):
    n = 2 * even.shape[1]
    lane = lax.broadcasted_iota(jnp.int32, even.shape, 1)
    weight = jnp.where((lane == 0) | (lane == n // 4), 1.0 / n, 2.0 / n)
    even = times_table(even * weight, table, 0, mm_t)
    odd = times_table(odd * (2.0 / n), table, 1, mm_t)
    return jnp.concatenate([even + odd, even - odd], axis=1)


def sublane_sums(parts):
    row = lax.broadcasted_iota(jnp.int32, parts[0].shape, 0)
    width = SUB // 2
    while width:
        low = (row & width) == 0
        merged = []
        for i in range(width):
            a, b = parts[i], parts[i + width]
            kept, moved = jnp.where(low, a, b), jnp.where(low, b, a)
            if 2 * width == SUB:
                moved = pltpu.roll(moved, width, 0)
            else:
                moved = jnp.where(low, pltpu.roll(moved, SUB - width, 0), pltpu.roll(moved, width, 0))
            merged.append(kept + moved)
        parts = merged
        width //= 2
    return parts[0]


def pack_rows(x):
    groups = x.shape[0] // SUB
    lane = lax.broadcasted_iota(jnp.int32, (SUB, LANES), 1)
    packed = x[:SUB]
    for i in range(1, groups):
        packed = jnp.where(lane >= i * (LANES // groups), x[i * SUB : (i + 1) * SUB], packed)
    return packed


def unpack_rows(packed, groups):
    step = LANES // groups
    return jnp.concatenate([packed[:, i * step : i * step + 1] for i in range(groups)], axis=0)


def lane_zero(shape):
    return lax.broadcasted_iota(jnp.int32, shape, len(shape) - 1) == 0


def even_forms(re, im):
    first = lane_zero(re.shape)
    return re, jnp.where(first, 0.0, im), jnp.where(first, im, re)


def spectra(counts, table):
    shape = counts.shape[:2]
    half = counts.shape[2] // 2
    return [
        mm(part.reshape(-1, half), table[2 * odd]).reshape(*shape, half)
        for odd, part in enumerate(fold(counts.astype(F32).astype(BF)))
    ]


def own_shells(step, share):
    groups = lax.axis_size("dp")
    return pl.multiple_of(lax.rem(lax.axis_index("dp") + step, groups) * share, SUB)


def expect_kernel(anneal, chunk, groups, frames, slices, table, *refs):
    count, shells, angles = frames.shape
    tilts = slices.shape[0]
    half, quarter = angles // 2, angles // 4
    chunks = count // chunk
    share = shells // groups
    rows = tilts * shells
    other, refs = refs[: groups - 1], refs[groups - 1 :]
    scores, local, own, fbuf, sbuf, tv, ya, yb, yc, cross, sems = refs
    spec = (own, *other)
    bases = [own_shells(s, share) for s in range(groups)]

    def frame_copy(c):
        at = pl.ds(c * chunk, chunk)
        return pltpu.make_async_copy(frames.at[at], fbuf.at[at], sems.at[2 + c])

    table_copy = pltpu.make_async_copy(table, tv, sems.at[0])
    slice_copy = pltpu.make_async_copy(slices, sbuf, sems.at[1])

    def transform(c):
        at = pl.ds(c * chunk, chunk)
        counts = jnp.concatenate([fbuf[at, pl.ds(base, share), :] for base in bases], axis=1)
        for odd, part in enumerate(spectra(counts, tv)):
            for s in range(groups):
                spec[s][at, :, odd * half : (odd + 1) * half] = part[:, s * share : (s + 1) * share]

    def correlate(c):
        out = pl.ds(c * SUB, SUB)
        for odd in range(2):
            for lanes in range(0, quarter, LANES):
                re_l = pl.ds(odd * half + lanes, LANES)
                im_l = pl.ds(odd * half + quarter + lanes, LANES)
                y_l = pl.ds(odd * quarter + lanes, LANES)
                sums = [[None] * SUB for _ in range(3)]
                for pair in range(0, chunk, 2):
                    for s in range(groups):
                        for g in range(share // SUB):
                            r = pl.ds(g * SUB, SUB)
                            ks = [c * chunk + pair + q for q in range(2)]
                            xs = [(spec[s][k, r, re_l], spec[s][k, r, im_l]) for k in ks]
                            xs = [(xr, xi, xr + xi) for xr, xi in xs]
                            for t in range(tilts):
                                y = pl.ds(bases[s] + (t * shells + g * SUB), SUB)
                                ys = ya[y, y_l], yb[y, y_l], yc[y, y_l]
                                for q in range(2):
                                    at = t * chunk + pair + q
                                    for i in range(3):
                                        u = xs[q][i] * ys[i]
                                        sums[i][at] = u if sums[i][at] is None else sums[i][at] + u
                m = [sublane_sums(part) for part in sums]
                re, im = m[0] + m[1], m[2] - m[0] + m[1]
                if lanes == 0 and not odd:
                    first = lane_zero(re.shape)
                    re, im = jnp.where(first, m[0], re), jnp.where(first, m[1], im)
                cross[out, re_l] = re
                cross[out, im_l] = im

    slice_copy.start()
    table_copy.start()
    for c in range(chunks):
        frame_copy(c).start()

    slice_copy.wait()
    logs = jnp.log(sbuf[...]).reshape(rows, angles)
    folded = fold(logs)
    dc = jnp.sum(logs, axis=1, keepdims=True)
    table_copy.wait()
    even, odd = [times_table(part, tv, i) for i, part in enumerate(folded)]
    even_re = jnp.where(lane_zero((rows, quarter)), dc, even[:, :quarter])
    for i, (re, im) in enumerate(((even_re, even[:, quarter:]), (odd[:, :quarter], odd[:, quarter:]))):
        at = slice(i * quarter, (i + 1) * quarter)
        ya[:, at] = re
        yb[:, at] = im
        yc[:, at] = re - im

    early = max(chunks - 2, 0)
    waits = {c: (c,) for c in range(early)} | {early: range(early, chunks)}
    for c in range(chunks):
        for later in waits.get(c, ()):
            frame_copy(later).wait()
        transform(c)
        if c < early:
            correlate(c)
    for c in range(early, chunks):
        correlate(c)

    spectrum = cross[...]
    dc = spectrum[:, :1]
    even = spectrum[:, :half]
    even = jnp.where(lane_zero(even.shape), 0.0, even)
    corr = from_half_spectrum(even, spectrum[:, half:], tv) + dc * (1.0 / angles)
    totals = [
        jnp.broadcast_to(jnp.sum(jnp.sum(sbuf[t], axis=0, keepdims=True), axis=1, keepdims=True), (chunk, 1))
        for t in range(tilts)
    ]
    part = anneal * (corr - jnp.concatenate(totals * chunks, axis=0))
    scores[...] = part

    def over_tilts(x, join):
        parts = []
        for c in range(chunks):
            group = x[c * SUB : (c + 1) * SUB]
            shift = chunk
            while shift < SUB:
                group = join(group, pltpu.roll(group, shift, 0))
                shift *= 2
            parts.append(group)
        return jnp.concatenate(parts, axis=0)

    wide = (tilts * count, LANES)
    top = over_tilts(jnp.broadcast_to(jnp.max(part, axis=1, keepdims=True), wide), jnp.maximum)
    total = jnp.sum(jnp.exp(part - top[:, :1]), axis=1, keepdims=True)
    local[...] = pack_rows(top + jnp.log(over_tilts(jnp.broadcast_to(total, wide), jnp.add)))


def in_hbm(x):
    return pltpu.with_memory_space_constraint(x, pltpu.HBM)


def expect(frames, slices, table, anneal, groups):
    count, shells, angles = frames.shape
    tilts = slices.shape[0]
    half = angles // 2
    chunk = SUB // tilts
    share = shells // groups
    hbm = pl.BlockSpec(memory_space=pltpu.HBM)
    vm = pl.BlockSpec(memory_space=pltpu.VMEM)
    form = pltpu.VMEM((tilts * shells, half), F32)
    *other, scores, local = pl.pallas_call(
        functools.partial(expect_kernel, anneal, chunk, groups),
        out_shape=(
            *[pltpu.VMEM((count, share, angles), F32)] * (groups - 1),
            pltpu.VMEM((tilts * count, angles), F32),
            pltpu.VMEM((SUB, LANES), F32),
        ),
        in_specs=[hbm] * 3,
        out_specs=(*[vm] * (groups - 1), vm, vm),
        scratch_shapes=[
            pltpu.VMEM((count, share, angles), F32),
            pltpu.VMEM((count, shells, angles), jnp.int32),
            pltpu.VMEM((tilts, shells, angles), F32),
            pltpu.VMEM(table.shape, BF),
            form,
            form,
            form,
            pltpu.VMEM((tilts * count, angles), F32),
            pltpu.SemaphoreType.DMA((2 + count // chunk,)),
        ],
        compiler_params=pltpu.CompilerParams(vmem_limit_bytes=VMEM_BYTES),
        name="expect",
    )(*(in_hbm(x) for x in (frames, slices, table)))
    return other, scores, local


def weights_kernel(scores, local, table, forms):
    own = jnp.exp(scores[...] - unpack_rows(local[...], scores.shape[0] // SUB))
    quarter = own.shape[1] // 4
    for odd, part in enumerate(to_half_spectrum(own, table)):
        re, im = part[:, :quarter], part[:, quarter:]
        at = slice(odd * quarter, (odd + 1) * quarter)
        forms[0, :, at] = re
        forms[1, :, at] = im
        forms[2, :, at] = re - im


def row_of(k, t, tilts):
    chunk = SUB // tilts
    return k // chunk * SUB + t * chunk + k % chunk


def back_project(first_tilt, spec, forms, local, lse, out, scaled):
    count, share, angles = spec.shape
    half, quarter = angles // 2, angles // 4
    sections = angles // LANES
    all_tilts = forms.shape[1] // count
    tilts = out.shape[0]
    factor = unpack_rows(jnp.exp(local[...] - lse[...]), all_tilts * count // SUB)
    scaled[...] = forms[...] * factor[None]
    for odd in range(2):
        for lanes in range(0, quarter, LANES):
            re_l = pl.ds(odd * half + lanes, LANES)
            im_l = pl.ds(odd * half + quarter + lanes, LANES)
            p_l = pl.ds(odd * quarter + lanes, LANES)
            for g in range(share // SUB):
                r = pl.ds(g * SUB, SUB)
                sums = [[None] * tilts for _ in range(3)]
                for k in range(count):
                    xr, xi = spec[k, r, re_l], spec[k, r, im_l]
                    xs = xr, xi, xr + xi
                    for t in range(tilts):
                        row = pl.ds(row_of(k, first_tilt + t, all_tilts), 1)
                        for i in range(3):
                            u = xs[i] * scaled[i, row, p_l]
                            sums[i][t] = u if k == 0 else sums[i][t] + u
                for t in range(tilts):
                    m = [part[t] for part in sums]
                    re, im = m[0] + m[1], m[2] - m[0] + m[1]
                    if lanes == 0 and not odd:
                        first = lane_zero(re.shape)
                        re, im = jnp.where(first, m[0], re), jnp.where(first, m[1], im)
                    out[t, pl.ds((odd * half + lanes) // LANES * share + g * SUB, SUB), :] = re
                    out[t, pl.ds((odd * half + quarter + lanes) // LANES * share + g * SUB, SUB), :] = im
    tilt_of = lax.broadcasted_iota(jnp.int32, (all_tilts * count, 1), 0) % SUB // (SUB // all_tilts)
    for t in range(tilts):
        weight = jnp.sum(jnp.where(tilt_of == first_tilt + t, scaled[0, :, :1], 0.0), axis=0, keepdims=True)
        out[t, pl.ds(sections * share, SUB), :] = jnp.broadcast_to(weight, (SUB, LANES))


def back_own_kernel(forms, local, lse, frames, table, out, counts, spec, scaled, sem):
    count, share, angles = spec.shape
    half = angles // 2
    copy = pltpu.make_async_copy(frames.at[:, pl.ds(own_shells(0, share), share), :], counts, sem)
    copy.start()
    copy.wait()
    chunk = min(count, 8)

    def step(c, carry):
        at = pl.ds(c * chunk, chunk)
        for odd, part in enumerate(spectra(counts[at], table)):
            spec[at, :, odd * half : (odd + 1) * half] = part
        return carry

    lax.fori_loop(0, count // chunk, step, 0)
    back_project(0, spec, forms, local, lse, out, scaled)


def back(shape, forms, local, lse, tilts, spec=None, frames=None, table=None):
    count, share, angles = shape
    half = angles // 2
    all_tilts = forms.shape[1] // count
    vm = pl.BlockSpec(memory_space=pltpu.VMEM)
    scaled = pltpu.VMEM(forms.shape, F32)
    call = functools.partial(
        pl.pallas_call,
        out_shape=pltpu.VMEM((len(tilts), share * (angles // LANES) + SUB, LANES), F32),
        out_specs=vm,
        compiler_params=pltpu.CompilerParams(vmem_limit_bytes=VMEM_BYTES),
        cost_estimate=pl.CostEstimate(
            flops=0 if spec is None else VECTOR_COST * 8 * count * len(tilts) * share * half,
            bytes_accessed=0 if spec is None else count * share * angles * 4,
            transcendentals=0,
        ),
    )
    if spec is not None:
        kernel = functools.partial(back_project, tilts[0])
        return call(kernel, in_specs=[vm] * 4, scratch_shapes=[scaled], name="back")(spec, forms, local, lse)
    return call(
        back_own_kernel,
        in_specs=[vm] * 3 + [pl.BlockSpec(memory_space=pltpu.HBM), vm],
        scratch_shapes=[
            pltpu.VMEM(shape, jnp.int32),
            pltpu.VMEM(shape, F32),
            scaled,
            pltpu.SemaphoreType.DMA,
        ],
        name="back_own",
    )(forms, local, lse, in_hbm(frames), table)


def log_kernel(scores, lse, after, out):
    count, tilts, _ = out.shape
    chunk = SUB // tilts
    value = scores[...] - unpack_rows(lse[...], scores.shape[0] // SUB)
    for c in range(count // chunk):
        for t in range(tilts):
            at = c * SUB + t * chunk
            out[pl.ds(c * chunk, chunk), t, :] = value[at : at + chunk]


def update_kernel(t, own, other, slices, table, *refs):
    out, result, sem = refs[-3:]
    share, angles = result.shape
    sections = angles // LANES

    def total(at):
        return own[t, at, :] + other[0, at, :]

    def columns(first, last):
        return jnp.concatenate([total(pl.ds(s * share, share)) for s in range(first, last)], axis=1)

    numer = from_half_spectrum(columns(0, sections // 2), columns(sections // 2, sections), table)
    weight = total(pl.ds(sections * share, 1))[:, :1]
    result[...] = (numer + slices[t, pl.ds(own_shells(0, share), share), :]) / (weight + 1.0)
    copy = pltpu.make_async_copy(result, out.at[t], sem)
    copy.start()
    copy.wait()


def update(t, own, other, slices, table, share, earlier):
    tilts, _, angles = slices.shape
    hbm = pl.BlockSpec(memory_space=pltpu.HBM)
    vm = pl.BlockSpec(memory_space=pltpu.VMEM)
    more = [] if earlier is None else [earlier]
    return pl.pallas_call(
        functools.partial(update_kernel, t),
        out_shape=jax.ShapeDtypeStruct((tilts, share, angles), F32),
        in_specs=[vm] * 4 + [hbm] * len(more),
        out_specs=hbm,
        scratch_shapes=[pltpu.VMEM((share, angles), F32), pltpu.SemaphoreType.DMA],
        input_output_aliases={4: 0} if more else {},
        compiler_params=pltpu.CompilerParams(vmem_limit_bytes=VMEM_BYTES),
        name="update",
    )(own, other, slices, table, *more)


def log_sum(a, b):
    return jnp.maximum(a, b) + jnp.log(1.0 + jnp.exp(-jnp.abs(a - b)))


def over_axis(value, axis):
    size = lax.axis_size(axis)
    if size & (size - 1):
        return jax.nn.logsumexp(lax.all_gather(value, axis), axis=0)
    bit = 1
    while bit < size:
        step = bit | 1
        value = log_sum(value, lax.ppermute(value, axis, [(i, i ^ step) for i in range(size)]))
        bit *= 2
    return value


def on_device(frames, slices):
    count, shells, angles = frames.shape
    tilts = slices.shape[0]
    anneal = 4.0 / math.sqrt(shells * angles)
    groups = lax.axis_size("dp")
    share = shells // groups
    table = jnp.asarray(spectrum_tables(angles))
    vm = pl.BlockSpec(memory_space=pltpu.VMEM)
    params = pltpu.CompilerParams(vmem_limit_bytes=VMEM_BYTES)

    spec, scores, local = expect(frames, slices, table, anneal, groups)
    forms = pl.pallas_call(
        weights_kernel,
        out_shape=pltpu.VMEM((3, tilts * count, angles // 2), F32),
        in_specs=[vm] * 3,
        out_specs=vm,
        compiler_params=params,
        cost_estimate=pl.CostEstimate(flops=3 * tilts * count * angles * angles, bytes_accessed=2 * angles * angles, transcendentals=0),
        name="transform",
    )(scores, local, table)
    lse = over_axis(local, "rot")

    shape = (count, share, angles)
    others = []
    for t in range(tilts):
        got = None
        for step in range(1, groups):
            block = back(shape, forms, local, lse, range(t, t + 1), spec=spec[step - 1])
            block = lax.ppermute(block, "dp", [(i, (i + step) % groups) for i in range(groups)])
            got = block if got is None else got + block
        others.append(got)
    own = back(shape, forms, local, lse, range(tilts), frames=frames, table=table)
    if groups == 1:
        others = [jnp.zeros_like(own[:1])] * tilts
    log_resp = pl.pallas_call(
        log_kernel,
        out_shape=jax.ShapeDtypeStruct((count, tilts, angles), F32),
        in_specs=[vm, vm, pl.BlockSpec(memory_space=pl.ANY)],
        out_specs=vm,
        compiler_params=params,
        name="log_resp",
    )(scores, lse, others[0])
    new_slices = None
    for t in range(tilts):
        new_slices = update(t, own, others[t], slices, table, share, new_slices)
    return (log_resp, new_slices)


def solution(mesh):
    in_specs = (P("dp", None, None), P("rot", None, None))
    out_specs = (P("dp", "rot", None), P("rot", "dp", None))
    return jax.shard_map(on_device, mesh=mesh, in_specs=in_specs, out_specs=out_specs, check_vma=False)
```

```python
import functools
import math

import jax
import jax.numpy as jnp
import ml_dtypes
import numpy as np
from jax import lax
from jax.experimental import pallas as pl
from jax.experimental.pallas import tpu as pltpu
from jax.sharding import PartitionSpec as P

BF = jnp.bfloat16
F32 = jnp.float32
LANES = 128
SUB = 8
VMEM_BYTES = 24 * 1024 * 1024
VECTOR_COST = 128


def spectrum_tables(n):
    half, quarter = n // 2, n // 4
    index = np.arange(half)
    pieces = []
    for odd in (0, 1):
        theta = (np.outer(index, 2 * np.arange(quarter) + odd) % n) * (2.0 * np.pi / n)
        table = np.concatenate([np.cos(theta), -np.sin(theta)], axis=1)
        if not odd:
            table[:, quarter] = np.where(index % 2 == 0, 1.0, -1.0)
        table = table.astype(np.float32)
        head = table.astype(ml_dtypes.bfloat16)
        pieces += [head, (table - head.astype(np.float32)).astype(ml_dtypes.bfloat16)]
    return np.stack(pieces)


def split2(x):
    head = x.astype(BF)
    return head, (x - head.astype(F32)).astype(BF)


def mm(a, b):
    return jnp.dot(a, b, preferred_element_type=F32)


def mm_t(a, b):
    return lax.dot_general(a, b, (((1,), (1,)), ((), ())), preferred_element_type=F32)


def times_table(x, table, odd, product=mm):
    rows = x.shape[0]
    x0, x1 = split2(x)
    both = product(jnp.concatenate([x0, x1], axis=0), table[2 * odd])
    return both[:rows] + (both[rows:] + product(x0, table[2 * odd + 1]))


def fold(x):
    half = x.shape[-1] // 2
    low, high = x[..., :half], x[..., half:]
    return low + high, low - high


def to_half_spectrum(x, table):
    return [times_table(part, table, odd) for odd, part in enumerate(fold(x))]


def from_half_spectrum(even, odd, table):
    n = 2 * even.shape[1]
    lane = lax.broadcasted_iota(jnp.int32, even.shape, 1)
    weight = jnp.where((lane == 0) | (lane == n // 4), 1.0 / n, 2.0 / n)
    even = times_table(even * weight, table, 0, mm_t)
    odd = times_table(odd * (2.0 / n), table, 1, mm_t)
    return jnp.concatenate([even + odd, even - odd], axis=1)


def sublane_sums(parts):
    row = lax.broadcasted_iota(jnp.int32, parts[0].shape, 0)
    width = SUB // 2
    while width:
        low = (row & width) == 0
        merged = []
        for i in range(width):
            a, b = parts[i], parts[i + width]
            kept, moved = jnp.where(low, a, b), jnp.where(low, b, a)
            if 2 * width == SUB:
                moved = pltpu.roll(moved, width, 0)
            else:
                moved = jnp.where(low, pltpu.roll(moved, SUB - width, 0), pltpu.roll(moved, width, 0))
            merged.append(kept + moved)
        parts = merged
        width //= 2
    return parts[0]


def frame_lanes(groups, tilts, group):
    frames = SUB // tilts
    step = LANES // (groups * frames)
    lane = lax.broadcasted_iota(jnp.int32, (SUB, LANES), 1)
    row = lax.broadcasted_iota(jnp.int32, (SUB, LANES), 0)
    return lane, (group * frames + row % frames) * step, step


def pack_rows(x, tilts):
    groups = x.shape[0] // SUB
    row = lax.broadcasted_iota(jnp.int32, (SUB, LANES), 0)
    packed = jnp.zeros((SUB, LANES), F32)
    for i in range(groups):
        lane, first, step = frame_lanes(groups, tilts, i)
        here = (lane >= first) & (lane < first + step) & (row < SUB // tilts)
        packed = jnp.where(here, x[i * SUB : (i + 1) * SUB], packed)
    return jnp.sum(packed, axis=0, keepdims=True)


def unpack_rows(packed, groups, tilts, width):
    wide = jnp.broadcast_to(packed, (SUB, LANES))
    rows = []
    for i in range(groups):
        _, first, _ = frame_lanes(groups, tilts, i)
        row = jnp.take_along_axis(wide, first, axis=1, mode="promise_in_bounds")
        rows.append(jnp.concatenate([row] * (width // LANES), axis=1))
    return jnp.concatenate(rows, axis=0)


def lane_zero(shape):
    return lax.broadcasted_iota(jnp.int32, shape, len(shape) - 1) == 0


def even_forms(re, im):
    first = lane_zero(re.shape)
    return re, jnp.where(first, 0.0, im), jnp.where(first, im, re)


def spectra(counts, table):
    shape = counts.shape[:2]
    half = counts.shape[2] // 2
    return [
        mm(part.reshape(-1, half), table[2 * odd]).reshape(*shape, half)
        for odd, part in enumerate(fold(counts.astype(F32).astype(BF)))
    ]


def own_shells(step, share):
    groups = lax.axis_size("dp")
    return pl.multiple_of(lax.rem(lax.axis_index("dp") + step, groups) * share, SUB)


def expect_kernel(anneal, chunk, groups, frames, slices, table, *refs):
    count, shells, angles = frames.shape
    tilts = slices.shape[0]
    half, quarter = angles // 2, angles // 4
    chunks = count // chunk
    share = shells // groups
    rows = tilts * shells
    other, refs = refs[: groups - 1], refs[groups - 1 :]
    scores, local, own, fbuf, sbuf, tv, ya, yb, yc, cross, sems = refs
    spec = (own, *other)
    bases = [own_shells(s, share) for s in range(groups)]

    def frame_copy(c):
        at = pl.ds(c * chunk, chunk)
        return pltpu.make_async_copy(frames.at[at], fbuf.at[at], sems.at[2 + c])

    table_copy = pltpu.make_async_copy(table, tv, sems.at[0])
    slice_copy = pltpu.make_async_copy(slices, sbuf, sems.at[1])

    def transform(c):
        at = pl.ds(c * chunk, chunk)
        counts = jnp.concatenate([fbuf[at, pl.ds(base, share), :] for base in bases], axis=1)
        for odd, part in enumerate(spectra(counts, tv)):
            for s in range(groups):
                spec[s][at, :, odd * half : (odd + 1) * half] = part[:, s * share : (s + 1) * share]

    def correlate(c):
        out = pl.ds(c * SUB, SUB)
        for odd in range(2):
            for lanes in range(0, quarter, LANES):
                re_l = pl.ds(odd * half + lanes, LANES)
                im_l = pl.ds(odd * half + quarter + lanes, LANES)
                y_l = pl.ds(odd * quarter + lanes, LANES)
                sums = [[None] * SUB for _ in range(3)]
                for pair in range(0, chunk, 2):
                    for s in range(groups):
                        for g in range(share // SUB):
                            r = pl.ds(g * SUB, SUB)
                            ks = [c * chunk + pair + q for q in range(2)]
                            xs = [(spec[s][k, r, re_l], spec[s][k, r, im_l]) for k in ks]
                            xs = [(xr, xi, xr + xi) for xr, xi in xs]
                            for t in range(tilts):
                                y = pl.ds(bases[s] + (t * shells + g * SUB), SUB)
                                ys = ya[y, y_l], yb[y, y_l], yc[y, y_l]
                                for q in range(2):
                                    at = t * chunk + pair + q
                                    for i in range(3):
                                        u = xs[q][i] * ys[i]
                                        sums[i][at] = u if sums[i][at] is None else sums[i][at] + u
                m = [sublane_sums(part) for part in sums]
                re, im = m[0] + m[1], m[2] - m[0] + m[1]
                if lanes == 0 and not odd:
                    first = lane_zero(re.shape)
                    re, im = jnp.where(first, m[0], re), jnp.where(first, m[1], im)
                cross[out, re_l] = re
                cross[out, im_l] = im

    slice_copy.start()
    table_copy.start()
    for c in range(chunks):
        frame_copy(c).start()

    slice_copy.wait()
    logs = jnp.log(sbuf[...]).reshape(rows, angles)
    folded = fold(logs)
    dc = jnp.sum(logs, axis=1, keepdims=True)
    table_copy.wait()
    even, odd = [times_table(part, tv, i) for i, part in enumerate(folded)]
    even_re = jnp.where(lane_zero((rows, quarter)), dc, even[:, :quarter])
    for i, (re, im) in enumerate(((even_re, even[:, quarter:]), (odd[:, :quarter], odd[:, quarter:]))):
        at = slice(i * quarter, (i + 1) * quarter)
        ya[:, at] = re
        yb[:, at] = im
        yc[:, at] = re - im

    early = max(chunks - 2, 0)
    waits = {c: (c,) for c in range(early)} | {early: range(early, chunks)}
    for c in range(chunks):
        for later in waits.get(c, ()):
            frame_copy(later).wait()
        transform(c)
        if c < early:
            correlate(c)
    for c in range(early, chunks):
        correlate(c)

    spectrum = cross[...]
    dc = spectrum[:, :1]
    even = spectrum[:, :half]
    even = jnp.where(lane_zero(even.shape), 0.0, even)
    corr = from_half_spectrum(even, spectrum[:, half:], tv) + dc * (1.0 / angles)
    totals = [
        jnp.broadcast_to(jnp.sum(jnp.sum(sbuf[t], axis=0, keepdims=True), axis=1, keepdims=True), (chunk, 1))
        for t in range(tilts)
    ]
    part = anneal * (corr - jnp.concatenate(totals * chunks, axis=0))
    scores[...] = part

    def over_tilts(x, join):
        parts = []
        for c in range(chunks):
            group = x[c * SUB : (c + 1) * SUB]
            shift = chunk
            while shift < SUB:
                group = join(group, pltpu.roll(group, shift, 0))
                shift *= 2
            parts.append(group)
        return jnp.concatenate(parts, axis=0)

    wide = (tilts * count, LANES)
    top = over_tilts(jnp.broadcast_to(jnp.max(part, axis=1, keepdims=True), wide), jnp.maximum)
    total = jnp.sum(jnp.exp(part - top[:, :1]), axis=1, keepdims=True)
    local[...] = pack_rows(top + jnp.log(over_tilts(jnp.broadcast_to(total, wide), jnp.add)), tilts)


def in_hbm(x):
    return pltpu.with_memory_space_constraint(x, pltpu.HBM)


def expect(frames, slices, table, anneal, groups):
    count, shells, angles = frames.shape
    tilts = slices.shape[0]
    half = angles // 2
    chunk = SUB // tilts
    share = shells // groups
    hbm = pl.BlockSpec(memory_space=pltpu.HBM)
    vm = pl.BlockSpec(memory_space=pltpu.VMEM)
    form = pltpu.VMEM((tilts * shells, half), F32)
    *other, scores, local = pl.pallas_call(
        functools.partial(expect_kernel, anneal, chunk, groups),
        out_shape=(
            *[pltpu.VMEM((count, share, angles), F32)] * (groups - 1),
            pltpu.VMEM((tilts * count, angles), F32),
            pltpu.VMEM((1, LANES), F32),
        ),
        in_specs=[hbm] * 3,
        out_specs=(*[vm] * (groups - 1), vm, vm),
        scratch_shapes=[
            pltpu.VMEM((count, share, angles), F32),
            pltpu.VMEM((count, shells, angles), jnp.int32),
            pltpu.VMEM((tilts, shells, angles), F32),
            pltpu.VMEM(table.shape, BF),
            form,
            form,
            form,
            pltpu.VMEM((tilts * count, angles), F32),
            pltpu.SemaphoreType.DMA((2 + count // chunk,)),
        ],
        compiler_params=pltpu.CompilerParams(vmem_limit_bytes=VMEM_BYTES),
        name="expect",
    )(*(in_hbm(x) for x in (frames, slices, table)))
    return other, scores, local


def weights_kernel(tilts, scores, local, table, forms):
    own = jnp.exp(scores[...] - unpack_rows(local[...], scores.shape[0] // SUB, tilts, scores.shape[1]))
    quarter = own.shape[1] // 4
    for odd, part in enumerate(to_half_spectrum(own, table)):
        re, im = part[:, :quarter], part[:, quarter:]
        at = slice(odd * quarter, (odd + 1) * quarter)
        forms[0, :, at] = re
        forms[1, :, at] = im
        forms[2, :, at] = re - im


def row_of(k, t, tilts):
    chunk = SUB // tilts
    return k // chunk * SUB + t * chunk + k % chunk


def back_project(first, spec, forms, local, lse, out, scaled):
    count, _, angles = spec.shape
    half, quarter = angles // 2, angles // 4
    sections = angles // LANES
    tilts = forms.shape[1] // count
    rows = out.shape[0] // SUB * SUB // sections // (SUB * tilts) * SUB
    factor = unpack_rows(jnp.exp(local[...] - lse[...]), tilts * count // SUB, tilts, half)
    scaled[...] = forms[...] * factor[None]
    for odd in range(2):
        for lanes in range(0, quarter, LANES):
            re_l = pl.ds(odd * half + lanes, LANES)
            im_l = pl.ds(odd * half + quarter + lanes, LANES)
            p_l = pl.ds(odd * quarter + lanes, LANES)
            for g in range(rows // SUB):
                r = pl.ds(first + g * SUB, SUB)
                sums = [[None] * tilts for _ in range(3)]
                for k in range(count):
                    xr, xi = spec[k, r, re_l], spec[k, r, im_l]
                    xs = xr, xi, xr + xi
                    for t in range(tilts):
                        row = pl.ds(row_of(k, t, tilts), 1)
                        for i in range(3):
                            u = xs[i] * scaled[i, row, p_l]
                            sums[i][t] = u if k == 0 else sums[i][t] + u
                for t in range(tilts):
                    m = [part[t] for part in sums]
                    re, im = m[0] + m[1], m[2] - m[0] + m[1]
                    if lanes == 0 and not odd:
                        first_lane = lane_zero(re.shape)
                        re, im = jnp.where(first_lane, m[0], re), jnp.where(first_lane, m[1], im)
                    at = t * rows + g * SUB
                    out[pl.ds((odd * half + lanes) // LANES * tilts * rows + at, SUB), :] = re
                    out[pl.ds((odd * half + quarter + lanes) // LANES * tilts * rows + at, SUB), :] = im
    if out.shape[0] > sections * tilts * rows:
        tilt_of = lax.broadcasted_iota(jnp.int32, (tilts * count, 1), 0) % SUB // (SUB // tilts)
        dc = scaled[0, :, :1]
        sums = [jnp.sum(jnp.where(tilt_of == t, dc, 0.0), axis=0, keepdims=True) for t in range(tilts)]
        tail = jnp.concatenate(sums + [jnp.zeros((SUB - tilts, 1), F32)], axis=0)
        out[pl.ds(sections * tilts * rows, SUB), :] = jnp.broadcast_to(tail, (SUB, LANES))


def back_signal_kernel(first, spec, forms, local, lse, table, out, scaled, half_spectrum):
    back_project(first, spec, forms, local, lse, half_spectrum, scaled)
    rows = out.shape[0]
    sections = out.shape[1] // LANES
    parts = [half_spectrum[pl.ds(s * rows, rows), :] for s in range(sections)]
    even = jnp.concatenate(parts[: sections // 2], axis=1)
    odd = jnp.concatenate(parts[sections // 2 :], axis=1)
    out[...] = from_half_spectrum(even, odd, table)


def back_own_kernel(forms, local, lse, frames, table, out, counts, spec, scaled, sem):
    count, share, angles = spec.shape
    half = angles // 2
    copy = pltpu.make_async_copy(frames.at[:, pl.ds(own_shells(0, share), share), :], counts, sem)
    copy.start()
    copy.wait()
    chunk = min(count, 8)

    def step(c, carry):
        at = pl.ds(c * chunk, chunk)
        for odd, part in enumerate(spectra(counts[at], table)):
            spec[at, :, odd * half : (odd + 1) * half] = part
        return carry

    lax.fori_loop(0, count // chunk, step, 0)
    back_project(0, spec, forms, local, lse, out, scaled)


def back(shape, forms, local, lse, first, rows, spec=None, frames=None, table=None):
    count, share, angles = shape
    half = angles // 2
    tilts = forms.shape[1] // count
    vm = pl.BlockSpec(memory_space=pltpu.VMEM)
    scaled = pltpu.VMEM(forms.shape, F32)
    call = functools.partial(
        pl.pallas_call,
        out_shape=pltpu.VMEM((tilts * rows * (angles // LANES) + (0 if first else SUB), LANES), F32),
        out_specs=vm,
        compiler_params=pltpu.CompilerParams(vmem_limit_bytes=VMEM_BYTES),
        cost_estimate=pl.CostEstimate(
            flops=0 if spec is None else VECTOR_COST * 8 * count * tilts * rows * half,
            bytes_accessed=0 if spec is None else count * rows * angles * 4,
            transcendentals=0,
        ),
    )
    if spec is not None:
        if table is None:
            kernel = functools.partial(back_project, first)
            return call(kernel, in_specs=[vm] * 4, scratch_shapes=[scaled], name="back")(spec, forms, local, lse)
        return call(
            functools.partial(back_signal_kernel, first),
            out_shape=pltpu.VMEM((tilts * rows, angles), F32),
            in_specs=[vm] * 5,
            scratch_shapes=[scaled, pltpu.VMEM((tilts * rows * (angles // LANES), LANES), F32)],
            name="back_signal",
        )(spec, forms, local, lse, table)
    return call(
        back_own_kernel,
        in_specs=[vm] * 3 + [pl.BlockSpec(memory_space=pltpu.HBM), vm],
        scratch_shapes=[
            pltpu.VMEM(shape, jnp.int32),
            pltpu.VMEM(shape, F32),
            scaled,
            pltpu.SemaphoreType.DMA,
        ],
        name="back_own",
    )(forms, local, lse, in_hbm(frames), table)


def log_kernel(scores, lse, after, out):
    count, tilts, _ = out.shape
    chunk = SUB // tilts
    value = scores[...] - unpack_rows(lse[...], scores.shape[0] // SUB, tilts, scores.shape[1])
    for c in range(count // chunk):
        for t in range(tilts):
            at = c * SUB + t * chunk
            out[pl.ds(c * chunk, chunk), t, :] = value[at : at + chunk]


def update_kernel(own, other, slices, table, out, rest, factor, result, sem):
    tilts, rows, angles = result.shape
    share = out.shape[1]
    sections = angles // LANES

    def numer(first, count, extra):
        columns = []
        for s in range(sections):
            mine = [own[pl.ds((s * tilts + t) * share + first, count), :] for t in range(tilts)]
            column = jnp.concatenate(mine, axis=0)
            columns.append(column + extra[pl.ds(s * tilts * count, tilts * count), :] if extra is not None else column)
        even = jnp.concatenate(columns[: sections // 2], axis=1)
        odd = jnp.concatenate(columns[sections // 2 :], axis=1)
        return from_half_spectrum(even, odd, table)

    at = [ref[pl.ds(ref.shape[0] - SUB, SUB), :] for ref in (own, other)]
    scale = 1.0 / (at[0] + at[1] + 1.0)
    base = own_shells(0, share)
    done = numer(0, rows, other)
    for t in range(tilts):
        before = slices[t, pl.ds(base, rows), :]
        result[t] = (done[t * rows : (t + 1) * rows] + before) * scale[t : t + 1, :1]
    copy = pltpu.make_async_copy(result, out.at[:, pl.ds(0, rows), :], sem)
    copy.start()
    left = share - rows
    part = numer(rows, left, None)
    for t in range(tilts):
        to = slice(t * left, (t + 1) * left)
        before = slices[t, pl.ds(base + rows, left), :]
        rest[to, :] = (part[to] + before) * scale[t : t + 1, :1]
        factor[to, :] = jnp.broadcast_to(scale[t : t + 1, :], (left, LANES))
    copy.wait()


def finish_kernel(other, rest, factor, earlier, out, result, sem):
    tilts, rows, angles = result.shape
    share = out.shape[1]
    for lanes in range(0, angles, LANES):
        at = pl.ds(lanes, LANES)
        result[:, :, at] = (other[:, at] * factor[...] + rest[:, at]).reshape(tilts, rows, LANES)
    copy = pltpu.make_async_copy(result, out.at[:, pl.ds(share - rows, rows), :], sem)
    copy.start()
    copy.wait()


def update(own, others, slices, table, share, rows):
    tilts, _, angles = slices.shape
    left = share - rows
    hbm = pl.BlockSpec(memory_space=pltpu.HBM)
    vm = pl.BlockSpec(memory_space=pltpu.VMEM)
    params = pltpu.CompilerParams(vmem_limit_bytes=VMEM_BYTES)
    whole = jax.ShapeDtypeStruct((tilts, share, angles), F32)
    new, rest, factor = pl.pallas_call(
        update_kernel,
        out_shape=(whole, pltpu.VMEM((tilts * left, angles), F32), pltpu.VMEM((tilts * left, LANES), F32)),
        in_specs=[vm] * 4,
        out_specs=(hbm, vm, vm),
        scratch_shapes=[pltpu.VMEM((tilts, rows, angles), F32), pltpu.SemaphoreType.DMA],
        compiler_params=params,
        name="update",
    )(own, others[0], slices, table)
    return pl.pallas_call(
        finish_kernel,
        out_shape=whole,
        in_specs=[vm] * 3 + [hbm],
        out_specs=hbm,
        scratch_shapes=[pltpu.VMEM((tilts, left, angles), F32), pltpu.SemaphoreType.DMA],
        input_output_aliases={3: 0},
        compiler_params=params,
        name="finish",
    )(others[1], rest, factor, new)


def log_sum(a, b):
    return jnp.maximum(a, b) + jnp.log(1.0 + jnp.exp(-jnp.abs(a - b)))


def over_axis(value, axis):
    size = lax.axis_size(axis)
    if size & (size - 1):
        return jax.nn.logsumexp(lax.all_gather(value, axis), axis=0)
    bit = 1
    while bit < size:
        step = bit | 1
        value = log_sum(value, lax.ppermute(value, axis, [(i, i ^ step) for i in range(size)]))
        bit *= 2
    return value


def on_device(frames, slices):
    count, shells, angles = frames.shape
    tilts = slices.shape[0]
    anneal = 4.0 / math.sqrt(shells * angles)
    groups = lax.axis_size("dp")
    share = shells // groups
    table = jnp.asarray(spectrum_tables(angles))
    vm = pl.BlockSpec(memory_space=pltpu.VMEM)
    params = pltpu.CompilerParams(vmem_limit_bytes=VMEM_BYTES)

    spec, scores, local = expect(frames, slices, table, anneal, groups)
    forms = pl.pallas_call(
        functools.partial(weights_kernel, tilts),
        out_shape=pltpu.VMEM((3, tilts * count, angles // 2), F32),
        in_specs=[vm] * 3,
        out_specs=vm,
        compiler_params=params,
        cost_estimate=pl.CostEstimate(flops=3 * tilts * count * angles * angles, bytes_accessed=2 * angles * angles, transcendentals=0),
        name="transform",
    )(scores, local, table)
    lse = over_axis(local, "rot")

    shape = (count, share, angles)
    rows = share // 2 // SUB * SUB
    others = []
    for first, shells_, signal in ((0, rows, None), (rows, share - rows, table)):
        got = None
        for step in range(1, groups):
            block = back(shape, forms, local, lse, first, shells_, spec=spec[step - 1], table=signal)
            block = lax.ppermute(block, "dp", [(i, (i + step) % groups) for i in range(groups)])
            got = block if got is None else got + block
        others.append(got)
    own = back(shape, forms, local, lse, 0, share, frames=frames, table=table)
    log_resp = pl.pallas_call(
        log_kernel,
        out_shape=jax.ShapeDtypeStruct((count, tilts, angles), F32),
        in_specs=[vm, vm, pl.BlockSpec(memory_space=pl.ANY)],
        out_specs=vm,
        compiler_params=params,
        name="log_resp",
    )(scores, lse, others[0])
    new_slices = update(own, others, slices, table, share, rows)
    return (log_resp, new_slices)


def solution(mesh):
    in_specs = (P("dp", None, None), P("rot", None, None))
    out_specs = (P("dp", "rot", None), P("rot", "dp", None))
    return jax.shard_map(on_device, mesh=mesh, in_specs=in_specs, out_specs=out_specs, check_vma=False)
```

```python
import functools
import math

import jax
import jax.numpy as jnp
import ml_dtypes
import numpy as np
from jax import lax
from jax.experimental import pallas as pl
from jax.experimental.pallas import tpu as pltpu
from jax.sharding import PartitionSpec as P

BF = jnp.bfloat16
F32 = jnp.float32
LANES = 128
SUB = 8
VMEM_BYTES = 24 * 1024 * 1024
VECTOR_COST = 128


def spectrum_tables(n):
    half, quarter = n // 2, n // 4
    index = np.arange(half)
    pieces = []
    for odd in (0, 1):
        theta = (np.outer(index, 2 * np.arange(quarter) + odd) % n) * (2.0 * np.pi / n)
        table = np.concatenate([np.cos(theta), -np.sin(theta)], axis=1)
        if not odd:
            table[:, quarter] = np.where(index % 2 == 0, 1.0, -1.0)
        table = table.astype(np.float32)
        head = table.astype(ml_dtypes.bfloat16)
        pieces += [head, (table - head.astype(np.float32)).astype(ml_dtypes.bfloat16)]
    return np.stack(pieces)


def split2(x):
    head = x.astype(BF)
    return head, (x - head.astype(F32)).astype(BF)


def mm(a, b):
    return jnp.dot(a, b, preferred_element_type=F32)


def mm_t(a, b):
    return lax.dot_general(a, b, (((1,), (1,)), ((), ())), preferred_element_type=F32)


def times_table(x, table, odd, product=mm):
    rows = x.shape[0]
    x0, x1 = split2(x)
    both = product(jnp.concatenate([x0, x1], axis=0), table[2 * odd])
    return both[:rows] + (both[rows:] + product(x0, table[2 * odd + 1]))


def fold(x):
    half = x.shape[-1] // 2
    low, high = x[..., :half], x[..., half:]
    return low + high, low - high


def to_half_spectrum(x, table):
    return [times_table(part, table, odd) for odd, part in enumerate(fold(x))]


def from_half_spectrum(even, odd, table):
    n = 2 * even.shape[1]
    lane = lax.broadcasted_iota(jnp.int32, even.shape, 1)
    weight = jnp.where((lane == 0) | (lane == n // 4), 1.0 / n, 2.0 / n)
    even = times_table(even * weight, table, 0, mm_t)
    odd = times_table(odd * (2.0 / n), table, 1, mm_t)
    return jnp.concatenate([even + odd, even - odd], axis=1)


def sublane_sums(parts):
    row = lax.broadcasted_iota(jnp.int32, parts[0].shape, 0)
    width = SUB // 2
    while width:
        low = (row & width) == 0
        merged = []
        for i in range(width):
            a, b = parts[i], parts[i + width]
            kept, moved = jnp.where(low, a, b), jnp.where(low, b, a)
            if 2 * width == SUB:
                moved = pltpu.roll(moved, width, 0)
            else:
                moved = jnp.where(low, pltpu.roll(moved, SUB - width, 0), pltpu.roll(moved, width, 0))
            merged.append(kept + moved)
        parts = merged
        width //= 2
    return parts[0]


def frame_lanes(groups, tilts, group):
    frames = SUB // tilts
    step = LANES // (groups * frames)
    lane = lax.broadcasted_iota(jnp.int32, (SUB, LANES), 1)
    row = lax.broadcasted_iota(jnp.int32, (SUB, LANES), 0)
    return lane, (group * frames + row % frames) * step, step


def pack_rows(x, tilts):
    groups = x.shape[0] // SUB
    row = lax.broadcasted_iota(jnp.int32, (SUB, LANES), 0)
    packed = jnp.zeros((SUB, LANES), F32)
    for i in range(groups):
        lane, first, step = frame_lanes(groups, tilts, i)
        here = (lane >= first) & (lane < first + step) & (row < SUB // tilts)
        packed = jnp.where(here, x[i * SUB : (i + 1) * SUB], packed)
    return jnp.sum(packed, axis=0, keepdims=True)


def unpack_rows(packed, groups, tilts, width):
    wide = jnp.broadcast_to(packed, (SUB, LANES))
    rows = []
    for i in range(groups):
        _, first, _ = frame_lanes(groups, tilts, i)
        row = jnp.take_along_axis(wide, first, axis=1, mode="promise_in_bounds")
        rows.append(jnp.concatenate([row] * (width // LANES), axis=1))
    return jnp.concatenate(rows, axis=0)


def lane_zero(shape):
    return lax.broadcasted_iota(jnp.int32, shape, len(shape) - 1) == 0


def even_forms(re, im):
    first = lane_zero(re.shape)
    return re, jnp.where(first, 0.0, im), jnp.where(first, im, re)


def spectra(counts, table):
    shape = counts.shape[:2]
    half = counts.shape[2] // 2
    return [
        mm(part.reshape(-1, half), table[2 * odd]).reshape(*shape, half)
        for odd, part in enumerate(fold(counts.astype(F32).astype(BF)))
    ]


def own_shells(step, share):
    groups = lax.axis_size("dp")
    return pl.multiple_of(lax.rem(lax.axis_index("dp") + step, groups) * share, SUB)


def expect_kernel(anneal, chunk, groups, frames, slices, table, *refs):
    count, shells, angles = frames.shape
    tilts = slices.shape[0]
    half, quarter = angles // 2, angles // 4
    chunks = count // chunk
    share = shells // groups
    rows = tilts * shells
    other, refs = refs[: groups - 1], refs[groups - 1 :]
    scores, local, own, fbuf, sbuf, tv, ya, yb, yc, cross, sems = refs
    spec = (own, *other)
    bases = [own_shells(s, share) for s in range(groups)]

    def frame_copy(c):
        at = pl.ds(c * chunk, chunk)
        return pltpu.make_async_copy(frames.at[at], fbuf.at[at], sems.at[2 + c])

    table_copy = pltpu.make_async_copy(table, tv, sems.at[0])
    slice_copy = pltpu.make_async_copy(slices, sbuf, sems.at[1])

    def transform(c):
        at = pl.ds(c * chunk, chunk)
        counts = jnp.concatenate([fbuf[at, pl.ds(base, share), :] for base in bases], axis=1)
        for odd, part in enumerate(spectra(counts, tv)):
            for s in range(groups):
                spec[s][at, :, odd * half : (odd + 1) * half] = part[:, s * share : (s + 1) * share]

    def correlate(c):
        out = pl.ds(c * SUB, SUB)
        for odd in range(2):
            for lanes in range(0, quarter, LANES):
                re_l = pl.ds(odd * half + lanes, LANES)
                im_l = pl.ds(odd * half + quarter + lanes, LANES)
                y_l = pl.ds(odd * quarter + lanes, LANES)
                sums = [[None] * SUB for _ in range(3)]
                for pair in range(0, chunk, 2):
                    for s in range(groups):
                        for g in range(share // SUB):
                            r = pl.ds(g * SUB, SUB)
                            ks = [c * chunk + pair + q for q in range(2)]
                            xs = [(spec[s][k, r, re_l], spec[s][k, r, im_l]) for k in ks]
                            xs = [(xr, xi, xr + xi) for xr, xi in xs]
                            for t in range(tilts):
                                y = pl.ds(bases[s] + (t * shells + g * SUB), SUB)
                                ys = ya[y, y_l], yb[y, y_l], yc[y, y_l]
                                for q in range(2):
                                    at = t * chunk + pair + q
                                    for i in range(3):
                                        u = xs[q][i] * ys[i]
                                        sums[i][at] = u if sums[i][at] is None else sums[i][at] + u
                m = [sublane_sums(part) for part in sums]
                re, im = m[0] + m[1], m[2] - m[0] + m[1]
                if lanes == 0 and not odd:
                    first = lane_zero(re.shape)
                    re, im = jnp.where(first, m[0], re), jnp.where(first, m[1], im)
                cross[out, re_l] = re
                cross[out, im_l] = im

    slice_copy.start()
    table_copy.start()
    for c in range(chunks):
        frame_copy(c).start()

    slice_copy.wait()
    logs = jnp.log(sbuf[...]).reshape(rows, angles)
    folded = fold(logs)
    dc = jnp.sum(logs, axis=1, keepdims=True)
    table_copy.wait()
    even, odd = [times_table(part, tv, i) for i, part in enumerate(folded)]
    even_re = jnp.where(lane_zero((rows, quarter)), dc, even[:, :quarter])
    for i, (re, im) in enumerate(((even_re, even[:, quarter:]), (odd[:, :quarter], odd[:, quarter:]))):
        at = slice(i * quarter, (i + 1) * quarter)
        ya[:, at] = re
        yb[:, at] = im
        yc[:, at] = re - im

    early = max(chunks - 2, 0)
    waits = {c: (c,) for c in range(early)} | {early: range(early, chunks)}
    for c in range(chunks):
        for later in waits.get(c, ()):
            frame_copy(later).wait()
        transform(c)
        if c < early:
            correlate(c)
    for c in range(early, chunks):
        correlate(c)

    spectrum = cross[...]
    dc = spectrum[:, :1]
    even = spectrum[:, :half]
    even = jnp.where(lane_zero(even.shape), 0.0, even)
    corr = from_half_spectrum(even, spectrum[:, half:], tv) + dc * (1.0 / angles)
    totals = [
        jnp.broadcast_to(jnp.sum(jnp.sum(sbuf[t], axis=0, keepdims=True), axis=1, keepdims=True), (chunk, 1))
        for t in range(tilts)
    ]
    part = anneal * (corr - jnp.concatenate(totals * chunks, axis=0))
    scores[...] = part

    def over_tilts(x, join):
        parts = []
        for c in range(chunks):
            group = x[c * SUB : (c + 1) * SUB]
            shift = chunk
            while shift < SUB:
                group = join(group, pltpu.roll(group, shift, 0))
                shift *= 2
            parts.append(group)
        return jnp.concatenate(parts, axis=0)

    wide = (tilts * count, LANES)
    top = over_tilts(jnp.broadcast_to(jnp.max(part, axis=1, keepdims=True), wide), jnp.maximum)
    total = jnp.sum(jnp.exp(part - top[:, :1]), axis=1, keepdims=True)
    local[...] = pack_rows(top + jnp.log(over_tilts(jnp.broadcast_to(total, wide), jnp.add)), tilts)


def in_hbm(x):
    return pltpu.with_memory_space_constraint(x, pltpu.HBM)


def expect(frames, slices, table, anneal, groups):
    count, shells, angles = frames.shape
    tilts = slices.shape[0]
    half = angles // 2
    chunk = SUB // tilts
    share = shells // groups
    hbm = pl.BlockSpec(memory_space=pltpu.HBM)
    vm = pl.BlockSpec(memory_space=pltpu.VMEM)
    form = pltpu.VMEM((tilts * shells, half), F32)
    *other, scores, local = pl.pallas_call(
        functools.partial(expect_kernel, anneal, chunk, groups),
        out_shape=(
            *[pltpu.VMEM((count, share, angles), F32)] * (groups - 1),
            pltpu.VMEM((tilts * count, angles), F32),
            pltpu.VMEM((1, LANES), F32),
        ),
        in_specs=[hbm] * 3,
        out_specs=(*[vm] * (groups - 1), vm, vm),
        scratch_shapes=[
            pltpu.VMEM((count, share, angles), F32),
            pltpu.VMEM((count, shells, angles), jnp.int32),
            pltpu.VMEM((tilts, shells, angles), F32),
            pltpu.VMEM(table.shape, BF),
            form,
            form,
            form,
            pltpu.VMEM((tilts * count, angles), F32),
            pltpu.SemaphoreType.DMA((2 + count // chunk,)),
        ],
        compiler_params=pltpu.CompilerParams(vmem_limit_bytes=VMEM_BYTES),
        name="expect",
    )(*(in_hbm(x) for x in (frames, slices, table)))
    return other, scores, local


def weights_kernel(tilts, scores, local, table, forms):
    own = jnp.exp(scores[...] - unpack_rows(local[...], scores.shape[0] // SUB, tilts, scores.shape[1]))
    quarter = own.shape[1] // 4
    for odd, part in enumerate(to_half_spectrum(own, table)):
        re, im = part[:, :quarter], part[:, quarter:]
        at = slice(odd * quarter, (odd + 1) * quarter)
        forms[0, :, at] = re
        forms[1, :, at] = im
        forms[2, :, at] = re - im


def row_of(k, t, tilts):
    chunk = SUB // tilts
    return k // chunk * SUB + t * chunk + k % chunk


def back_project(first, spec, forms, local, lse, out, scaled):
    count, _, angles = spec.shape
    half, quarter = angles // 2, angles // 4
    sections = angles // LANES
    tilts = forms.shape[1] // count
    rows = out.shape[0] // SUB * SUB // sections // (SUB * tilts) * SUB
    factor = unpack_rows(jnp.exp(local[...] - lse[...]), tilts * count // SUB, tilts, half)
    scaled[...] = forms[...] * factor[None]
    for odd in range(2):
        for lanes in range(0, quarter, LANES):
            re_l = pl.ds(odd * half + lanes, LANES)
            im_l = pl.ds(odd * half + quarter + lanes, LANES)
            p_l = pl.ds(odd * quarter + lanes, LANES)
            for g in range(rows // SUB):
                r = pl.ds(first + g * SUB, SUB)
                sums = [[None] * tilts for _ in range(3)]
                for k in range(count):
                    xr, xi = spec[k, r, re_l], spec[k, r, im_l]
                    xs = xr, xi, xr + xi
                    for t in range(tilts):
                        row = pl.ds(row_of(k, t, tilts), 1)
                        for i in range(3):
                            u = xs[i] * scaled[i, row, p_l]
                            sums[i][t] = u if k == 0 else sums[i][t] + u
                for t in range(tilts):
                    m = [part[t] for part in sums]
                    re, im = m[0] + m[1], m[2] - m[0] + m[1]
                    if lanes == 0 and not odd:
                        first_lane = lane_zero(re.shape)
                        re, im = jnp.where(first_lane, m[0], re), jnp.where(first_lane, m[1], im)
                    at = t * rows + g * SUB
                    out[pl.ds((odd * half + lanes) // LANES * tilts * rows + at, SUB), :] = re
                    out[pl.ds((odd * half + quarter + lanes) // LANES * tilts * rows + at, SUB), :] = im
    if out.shape[0] > sections * tilts * rows:
        tilt_of = lax.broadcasted_iota(jnp.int32, (tilts * count, 1), 0) % SUB // (SUB // tilts)
        dc = scaled[0, :, :1]
        sums = [jnp.sum(jnp.where(tilt_of == t, dc, 0.0), axis=0, keepdims=True) for t in range(tilts)]
        tail = jnp.concatenate(sums + [jnp.zeros((SUB - tilts, 1), F32)], axis=0)
        out[pl.ds(sections * tilts * rows, SUB), :] = jnp.broadcast_to(tail, (SUB, LANES))


def back_signal_kernel(first, spec, forms, local, lse, table, out, scaled, half_spectrum):
    back_project(first, spec, forms, local, lse, half_spectrum, scaled)
    rows = out.shape[0]
    sections = out.shape[1] // LANES
    parts = [half_spectrum[pl.ds(s * rows, rows), :] for s in range(sections)]
    even = jnp.concatenate(parts[: sections // 2], axis=1)
    odd = jnp.concatenate(parts[sections // 2 :], axis=1)
    out[...] = from_half_spectrum(even, odd, table)


def back_own_kernel(forms, local, lse, frames, table, out, counts, spec, scaled, sem):
    count, share, angles = spec.shape
    half = angles // 2
    copy = pltpu.make_async_copy(frames.at[:, pl.ds(own_shells(0, share), share), :], counts, sem)
    copy.start()
    copy.wait()
    chunk = min(count, 8)

    def step(c, carry):
        at = pl.ds(c * chunk, chunk)
        for odd, part in enumerate(spectra(counts[at], table)):
            spec[at, :, odd * half : (odd + 1) * half] = part
        return carry

    lax.fori_loop(0, count // chunk, step, 0)
    back_project(0, spec, forms, local, lse, out, scaled)


def back(shape, forms, local, lse, first, rows, spec=None, frames=None, table=None):
    count, share, angles = shape
    half = angles // 2
    tilts = forms.shape[1] // count
    vm = pl.BlockSpec(memory_space=pltpu.VMEM)
    scaled = pltpu.VMEM(forms.shape, F32)
    call = functools.partial(
        pl.pallas_call,
        out_shape=pltpu.VMEM((tilts * rows * (angles // LANES) + (0 if first else SUB), LANES), F32),
        out_specs=vm,
        compiler_params=pltpu.CompilerParams(vmem_limit_bytes=VMEM_BYTES),
        cost_estimate=pl.CostEstimate(
            flops=0 if spec is None else VECTOR_COST * 8 * count * tilts * rows * half,
            bytes_accessed=0 if spec is None else count * rows * angles * 4,
            transcendentals=0,
        ),
    )
    if spec is not None:
        if table is None:
            kernel = functools.partial(back_project, first)
            return call(kernel, in_specs=[vm] * 4, scratch_shapes=[scaled], name="back")(spec, forms, local, lse)
        return call(
            functools.partial(back_signal_kernel, first),
            out_shape=pltpu.VMEM((tilts * rows, angles), F32),
            in_specs=[vm] * 5,
            scratch_shapes=[scaled, pltpu.VMEM((tilts * rows * (angles // LANES), LANES), F32)],
            name="back_signal",
        )(spec, forms, local, lse, table)
    return call(
        back_own_kernel,
        in_specs=[vm] * 3 + [pl.BlockSpec(memory_space=pltpu.HBM), vm],
        scratch_shapes=[
            pltpu.VMEM(shape, jnp.int32),
            pltpu.VMEM(shape, F32),
            scaled,
            pltpu.SemaphoreType.DMA,
        ],
        name="back_own",
    )(forms, local, lse, in_hbm(frames), table)


def log_kernel(scores, lse, after, out):
    count, tilts, _ = out.shape
    chunk = SUB // tilts
    value = scores[...] - unpack_rows(lse[...], scores.shape[0] // SUB, tilts, scores.shape[1])
    for c in range(count // chunk):
        for t in range(tilts):
            at = c * SUB + t * chunk
            out[pl.ds(c * chunk, chunk), t, :] = value[at : at + chunk]


def update_kernel(own, other, slices, table, out, rest, factor, result, sem):
    tilts, rows, angles = result.shape
    share = out.shape[1]
    sections = angles // LANES

    def numer(first, count, extra):
        columns = []
        for s in range(sections):
            mine = [own[pl.ds((s * tilts + t) * share + first, count), :] for t in range(tilts)]
            column = jnp.concatenate(mine, axis=0)
            columns.append(column + extra[pl.ds(s * tilts * count, tilts * count), :] if extra is not None else column)
        even = jnp.concatenate(columns[: sections // 2], axis=1)
        odd = jnp.concatenate(columns[sections // 2 :], axis=1)
        return from_half_spectrum(even, odd, table)

    at = [ref[pl.ds(ref.shape[0] - SUB, SUB), :] for ref in (own, other)]
    scale = 1.0 / (at[0] + at[1] + 1.0)
    base = own_shells(0, share)
    done = numer(0, rows, other)
    for t in range(tilts):
        before = slices[t, pl.ds(base, rows), :]
        result[t] = (done[t * rows : (t + 1) * rows] + before) * scale[t : t + 1, :1]
    copy = pltpu.make_async_copy(result, out.at[:, pl.ds(0, rows), :], sem)
    copy.start()
    left = share - rows
    part = numer(rows, left, None)
    for t in range(tilts):
        to = slice(t * left, (t + 1) * left)
        before = slices[t, pl.ds(base + rows, left), :]
        rest[to, :] = (part[to] + before) * scale[t : t + 1, :1]
        factor[to, :] = jnp.broadcast_to(scale[t : t + 1, :], (left, LANES))
    copy.wait()


def finish_kernel(other, rest, factor, earlier, out, result, sem):
    tilts, rows, angles = result.shape
    share = out.shape[1]
    for lanes in range(0, angles, LANES):
        at = pl.ds(lanes, LANES)
        result[:, :, at] = (other[:, at] * factor[...] + rest[:, at]).reshape(tilts, rows, LANES)
    copy = pltpu.make_async_copy(result, out.at[:, pl.ds(share - rows, rows), :], sem)
    copy.start()
    copy.wait()


def update(own, others, slices, table, share, rows):
    tilts, _, angles = slices.shape
    left = share - rows
    hbm = pl.BlockSpec(memory_space=pltpu.HBM)
    vm = pl.BlockSpec(memory_space=pltpu.VMEM)
    params = pltpu.CompilerParams(vmem_limit_bytes=VMEM_BYTES)
    whole = jax.ShapeDtypeStruct((tilts, share, angles), F32)
    new, rest, factor = pl.pallas_call(
        update_kernel,
        out_shape=(whole, pltpu.VMEM((tilts * left, angles), F32), pltpu.VMEM((tilts * left, LANES), F32)),
        in_specs=[vm] * 4,
        out_specs=(hbm, vm, vm),
        scratch_shapes=[pltpu.VMEM((tilts, rows, angles), F32), pltpu.SemaphoreType.DMA],
        compiler_params=params,
        name="update",
    )(own, others[0], slices, table)
    return pl.pallas_call(
        finish_kernel,
        out_shape=whole,
        in_specs=[vm] * 3 + [hbm],
        out_specs=hbm,
        scratch_shapes=[pltpu.VMEM((tilts, left, angles), F32), pltpu.SemaphoreType.DMA],
        input_output_aliases={3: 0},
        compiler_params=params,
        name="finish",
    )(others[1], rest, factor, new)


def log_sum(values):
    top = functools.reduce(jnp.maximum, values)
    return top + jnp.log(sum(jnp.exp(value - top) for value in values))


def over_axis(value, axis):
    size = lax.axis_size(axis)
    if size & (size - 1):
        return jax.nn.logsumexp(lax.all_gather(value, axis), axis=0)
    bits = [1 << i for i in range(size.bit_length() - 1)]
    rounds = [[bit] for bit in bits[:1]] + [bits[i : i + 2] for i in range(1, len(bits), 2)]
    for bits in rounds:
        steps = [step | 1 for step in ([*bits, sum(bits)] if len(bits) == 2 else bits)]
        parts = [lax.ppermute(value, axis, [(i, i ^ step) for i in range(size)]) for step in steps]
        value = log_sum([value, *parts])
    return value


def on_device(frames, slices):
    count, shells, angles = frames.shape
    tilts = slices.shape[0]
    anneal = 4.0 / math.sqrt(shells * angles)
    groups = lax.axis_size("dp")
    share = shells // groups
    table = jnp.asarray(spectrum_tables(angles))
    vm = pl.BlockSpec(memory_space=pltpu.VMEM)
    params = pltpu.CompilerParams(vmem_limit_bytes=VMEM_BYTES)

    spec, scores, local = expect(frames, slices, table, anneal, groups)
    forms = pl.pallas_call(
        functools.partial(weights_kernel, tilts),
        out_shape=pltpu.VMEM((3, tilts * count, angles // 2), F32),
        in_specs=[vm] * 3,
        out_specs=vm,
        compiler_params=params,
        cost_estimate=pl.CostEstimate(flops=3 * tilts * count * angles * angles, bytes_accessed=2 * angles * angles, transcendentals=0),
        name="transform",
    )(scores, local, table)
    lse = over_axis(local, "rot")

    shape = (count, share, angles)
    rows = share // 2 // SUB * SUB
    others = []
    for first, shells_, signal in ((0, rows, None), (rows, share - rows, table)):
        got = None
        for step in range(1, groups):
            block = back(shape, forms, local, lse, first, shells_, spec=spec[step - 1], table=signal)
            block = lax.ppermute(block, "dp", [(i, (i + step) % groups) for i in range(groups)])
            got = block if got is None else got + block
        others.append(got)
    own = back(shape, forms, local, lse, 0, share, frames=frames, table=table)
    log_resp = pl.pallas_call(
        log_kernel,
        out_shape=jax.ShapeDtypeStruct((count, tilts, angles), F32),
        in_specs=[vm, vm, pl.BlockSpec(memory_space=pl.ANY)],
        out_specs=vm,
        compiler_params=params,
        name="log_resp",
    )(scores, lse, others[0])
    new_slices = update(own, others, slices, table, share, rows)
    return (log_resp, new_slices)


def solution(mesh):
    in_specs = (P("dp", None, None), P("rot", None, None))
    out_specs = (P("dp", "rot", None), P("rot", "dp", None))
    return jax.shard_map(on_device, mesh=mesh, in_specs=in_specs, out_specs=out_specs, check_vma=False)
```

```python
import functools
import math

import jax
import jax.numpy as jnp
import ml_dtypes
import numpy as np
from jax import lax
from jax.experimental import pallas as pl
from jax.experimental.pallas import tpu as pltpu
from jax.sharding import PartitionSpec as P

BF = jnp.bfloat16
F32 = jnp.float32
LANES = 128
SUB = 8
VMEM_BYTES = 24 * 1024 * 1024
VECTOR_COST = 128


def spectrum_tables(n):
    half, quarter = n // 2, n // 4
    index = np.arange(half)
    pieces = []
    for odd in (0, 1):
        theta = (np.outer(index, 2 * np.arange(quarter) + odd) % n) * (2.0 * np.pi / n)
        table = np.concatenate([np.cos(theta), -np.sin(theta)], axis=1)
        if not odd:
            table[:, quarter] = np.where(index % 2 == 0, 1.0, -1.0)
        table = table.astype(np.float32)
        head = table.astype(ml_dtypes.bfloat16)
        pieces += [head, (table - head.astype(np.float32)).astype(ml_dtypes.bfloat16)]
    return np.stack(pieces)


def split2(x):
    head = x.astype(BF)
    return head, (x - head.astype(F32)).astype(BF)


def mm(a, b):
    return jnp.dot(a, b, preferred_element_type=F32)


def mm_t(a, b):
    return lax.dot_general(a, b, (((1,), (1,)), ((), ())), preferred_element_type=F32)


def times_table(x, table, odd, product=mm):
    rows = x.shape[0]
    x0, x1 = split2(x)
    both = product(jnp.concatenate([x0, x1], axis=0), table[2 * odd])
    return both[:rows] + (both[rows:] + product(x0, table[2 * odd + 1]))


def fold(x):
    half = x.shape[-1] // 2
    low, high = x[..., :half], x[..., half:]
    return low + high, low - high


def to_half_spectrum(x, table):
    return [times_table(part, table, odd) for odd, part in enumerate(fold(x))]


def from_half_spectrum(even, odd, table):
    n = 2 * even.shape[1]
    lane = lax.broadcasted_iota(jnp.int32, even.shape, 1)
    weight = jnp.where((lane == 0) | (lane == n // 4), 1.0 / n, 2.0 / n)
    even = times_table(even * weight, table, 0, mm_t)
    odd = times_table(odd * (2.0 / n), table, 1, mm_t)
    return jnp.concatenate([even + odd, even - odd], axis=1)


def sublane_sums(parts):
    row = lax.broadcasted_iota(jnp.int32, parts[0].shape, 0)
    width = SUB // 2
    while width:
        low = (row & width) == 0
        merged = []
        for i in range(width):
            a, b = parts[i], parts[i + width]
            kept, moved = jnp.where(low, a, b), jnp.where(low, b, a)
            if 2 * width == SUB:
                moved = pltpu.roll(moved, width, 0)
            else:
                moved = jnp.where(low, pltpu.roll(moved, SUB - width, 0), pltpu.roll(moved, width, 0))
            merged.append(kept + moved)
        parts = merged
        width //= 2
    return parts[0]


def frame_lanes(groups, tilts, group):
    frames = SUB // tilts
    step = LANES // (groups * frames)
    lane = lax.broadcasted_iota(jnp.int32, (SUB, LANES), 1)
    row = lax.broadcasted_iota(jnp.int32, (SUB, LANES), 0)
    return lane, (group * frames + row % frames) * step, step


def pack_rows(x, tilts):
    groups = x.shape[0] // SUB
    row = lax.broadcasted_iota(jnp.int32, (SUB, LANES), 0)
    packed = jnp.zeros((SUB, LANES), F32)
    for i in range(groups):
        lane, first, step = frame_lanes(groups, tilts, i)
        here = (lane >= first) & (lane < first + step) & (row < SUB // tilts)
        packed = jnp.where(here, x[i * SUB : (i + 1) * SUB], packed)
    return jnp.sum(packed, axis=0, keepdims=True)


def unpack_rows(packed, groups, tilts, width):
    wide = jnp.broadcast_to(packed, (SUB, LANES))
    rows = []
    for i in range(groups):
        _, first, _ = frame_lanes(groups, tilts, i)
        row = jnp.take_along_axis(wide, first, axis=1, mode="promise_in_bounds")
        rows.append(jnp.concatenate([row] * (width // LANES), axis=1))
    return jnp.concatenate(rows, axis=0)


def lane_zero(shape):
    return lax.broadcasted_iota(jnp.int32, shape, len(shape) - 1) == 0


def even_forms(re, im):
    first = lane_zero(re.shape)
    return re, jnp.where(first, 0.0, im), jnp.where(first, im, re)


def spectra(counts, table):
    shape = counts.shape[:2]
    half = counts.shape[2] // 2
    return [
        mm(part.reshape(-1, half), table[2 * odd]).reshape(*shape, half)
        for odd, part in enumerate(fold(counts.astype(F32).astype(BF)))
    ]


def own_shells(step, share):
    groups = lax.axis_size("dp")
    return pl.multiple_of(lax.rem(lax.axis_index("dp") + step, groups) * share, SUB)


def expect_kernel(anneal, chunk, groups, frames, slices, table, *refs):
    count, shells, angles = frames.shape
    tilts = slices.shape[0]
    half, quarter = angles // 2, angles // 4
    chunks = count // chunk
    share = shells // groups
    rows = tilts * shells
    other, refs = refs[: groups - 1], refs[groups - 1 :]
    scores, local, tv, own, fbuf, sbuf, ya, yb, yc, cross, sems = refs
    spec = (own, *other)
    bases = [own_shells(s, share) for s in range(groups)]

    def frame_copy(c):
        at = pl.ds(c * chunk, chunk)
        return pltpu.make_async_copy(frames.at[at], fbuf.at[at], sems.at[2 + c])

    table_copy = pltpu.make_async_copy(table, tv, sems.at[0])
    slice_copy = pltpu.make_async_copy(slices, sbuf, sems.at[1])

    def transform(c):
        at = pl.ds(c * chunk, chunk)
        counts = jnp.concatenate([fbuf[at, pl.ds(base, share), :] for base in bases], axis=1)
        for odd, part in enumerate(spectra(counts, tv)):
            for s in range(groups):
                spec[s][at, :, odd * half : (odd + 1) * half] = part[:, s * share : (s + 1) * share]

    def correlate(c):
        out = pl.ds(c * SUB, SUB)
        for odd in range(2):
            for lanes in range(0, quarter, LANES):
                re_l = pl.ds(odd * half + lanes, LANES)
                im_l = pl.ds(odd * half + quarter + lanes, LANES)
                y_l = pl.ds(odd * quarter + lanes, LANES)
                sums = [[None] * SUB for _ in range(3)]
                for pair in range(0, chunk, 2):
                    for s in range(groups):
                        for g in range(share // SUB):
                            r = pl.ds(g * SUB, SUB)
                            ks = [c * chunk + pair + q for q in range(2)]
                            xs = [(spec[s][k, r, re_l], spec[s][k, r, im_l]) for k in ks]
                            xs = [(xr, xi, xr + xi) for xr, xi in xs]
                            for t in range(tilts):
                                y = pl.ds(bases[s] + (t * shells + g * SUB), SUB)
                                ys = ya[y, y_l], yb[y, y_l], yc[y, y_l]
                                for q in range(2):
                                    at = t * chunk + pair + q
                                    for i in range(3):
                                        u = xs[q][i] * ys[i]
                                        sums[i][at] = u if sums[i][at] is None else sums[i][at] + u
                m = [sublane_sums(part) for part in sums]
                re, im = m[0] + m[1], m[2] - m[0] + m[1]
                if lanes == 0 and not odd:
                    first = lane_zero(re.shape)
                    re, im = jnp.where(first, m[0], re), jnp.where(first, m[1], im)
                cross[out, re_l] = re
                cross[out, im_l] = im

    slice_copy.start()
    table_copy.start()
    for c in range(chunks):
        frame_copy(c).start()

    slice_copy.wait()
    logs = jnp.log(sbuf[...]).reshape(rows, angles)
    folded = fold(logs)
    dc = jnp.sum(logs, axis=1, keepdims=True)
    table_copy.wait()
    even, odd = [times_table(part, tv, i) for i, part in enumerate(folded)]
    even_re = jnp.where(lane_zero((rows, quarter)), dc, even[:, :quarter])
    for i, (re, im) in enumerate(((even_re, even[:, quarter:]), (odd[:, :quarter], odd[:, quarter:]))):
        at = slice(i * quarter, (i + 1) * quarter)
        ya[:, at] = re
        yb[:, at] = im
        yc[:, at] = re - im

    early = max(chunks - 2, 0)
    waits = {c: (c,) for c in range(early)} | {early: range(early, chunks)}
    for c in range(chunks):
        for later in waits.get(c, ()):
            frame_copy(later).wait()
        transform(c)
        if c < early:
            correlate(c)
    for c in range(early, chunks):
        correlate(c)

    spectrum = cross[...]
    dc = spectrum[:, :1]
    even = spectrum[:, :half]
    even = jnp.where(lane_zero(even.shape), 0.0, even)
    corr = from_half_spectrum(even, spectrum[:, half:], tv) + dc * (1.0 / angles)
    totals = [
        jnp.broadcast_to(jnp.sum(jnp.sum(sbuf[t], axis=0, keepdims=True), axis=1, keepdims=True), (chunk, 1))
        for t in range(tilts)
    ]
    part = anneal * (corr - jnp.concatenate(totals * chunks, axis=0))
    scores[...] = part

    def over_tilts(x, join):
        parts = []
        for c in range(chunks):
            group = x[c * SUB : (c + 1) * SUB]
            shift = chunk
            while shift < SUB:
                group = join(group, pltpu.roll(group, shift, 0))
                shift *= 2
            parts.append(group)
        return jnp.concatenate(parts, axis=0)

    wide = (tilts * count, LANES)
    top = over_tilts(jnp.broadcast_to(jnp.max(part, axis=1, keepdims=True), wide), jnp.maximum)
    total = jnp.sum(jnp.exp(part - top[:, :1]), axis=1, keepdims=True)
    local[...] = pack_rows(top + jnp.log(over_tilts(jnp.broadcast_to(total, wide), jnp.add)), tilts)


def in_hbm(x):
    return pltpu.with_memory_space_constraint(x, pltpu.HBM)


def expect(frames, slices, table, anneal, groups):
    count, shells, angles = frames.shape
    tilts = slices.shape[0]
    half = angles // 2
    chunk = SUB // tilts
    share = shells // groups
    hbm = pl.BlockSpec(memory_space=pltpu.HBM)
    vm = pl.BlockSpec(memory_space=pltpu.VMEM)
    form = pltpu.VMEM((tilts * shells, half), F32)
    *other, scores, local, table = pl.pallas_call(
        functools.partial(expect_kernel, anneal, chunk, groups),
        out_shape=(
            *[pltpu.VMEM((count, share, angles), F32)] * (groups - 1),
            pltpu.VMEM((tilts * count, angles), F32),
            pltpu.VMEM((1, LANES), F32),
            pltpu.VMEM(table.shape, BF),
        ),
        in_specs=[hbm] * 3,
        out_specs=(*[vm] * (groups - 1), vm, vm, vm),
        scratch_shapes=[
            pltpu.VMEM((count, share, angles), F32),
            pltpu.VMEM((count, shells, angles), jnp.int32),
            pltpu.VMEM((tilts, shells, angles), F32),
            form,
            form,
            form,
            pltpu.VMEM((tilts * count, angles), F32),
            pltpu.SemaphoreType.DMA((2 + count // chunk,)),
        ],
        compiler_params=pltpu.CompilerParams(vmem_limit_bytes=VMEM_BYTES),
        name="expect",
    )(*(in_hbm(x) for x in (frames, slices, table)))
    return other, scores, local, table


def weights_kernel(tilts, scores, local, table, forms):
    own = jnp.exp(scores[...] - unpack_rows(local[...], scores.shape[0] // SUB, tilts, scores.shape[1]))
    quarter = own.shape[1] // 4
    for odd, part in enumerate(to_half_spectrum(own, table)):
        re, im = part[:, :quarter], part[:, quarter:]
        at = slice(odd * quarter, (odd + 1) * quarter)
        forms[0, :, at] = re
        forms[1, :, at] = im
        forms[2, :, at] = re - im


def row_of(k, t, tilts):
    chunk = SUB // tilts
    return k // chunk * SUB + t * chunk + k % chunk


def back_project(first, spec, forms, local, lse, out, scaled):
    count, _, angles = spec.shape
    half, quarter = angles // 2, angles // 4
    sections = angles // LANES
    tilts = forms.shape[1] // count
    rows = out.shape[0] // SUB * SUB // sections // (SUB * tilts) * SUB
    factor = unpack_rows(jnp.exp(local[...] - lse[...]), tilts * count // SUB, tilts, half)
    scaled[...] = forms[...] * factor[None]
    for odd in range(2):
        for lanes in range(0, quarter, LANES):
            re_l = pl.ds(odd * half + lanes, LANES)
            im_l = pl.ds(odd * half + quarter + lanes, LANES)
            p_l = pl.ds(odd * quarter + lanes, LANES)
            for g in range(rows // SUB):
                r = pl.ds(first + g * SUB, SUB)
                sums = [[None] * tilts for _ in range(3)]
                for k in range(count):
                    xr, xi = spec[k, r, re_l], spec[k, r, im_l]
                    xs = xr, xi, xr + xi
                    for t in range(tilts):
                        row = pl.ds(row_of(k, t, tilts), 1)
                        for i in range(3):
                            u = xs[i] * scaled[i, row, p_l]
                            sums[i][t] = u if k == 0 else sums[i][t] + u
                for t in range(tilts):
                    m = [part[t] for part in sums]
                    re, im = m[0] + m[1], m[2] - m[0] + m[1]
                    if lanes == 0 and not odd:
                        first_lane = lane_zero(re.shape)
                        re, im = jnp.where(first_lane, m[0], re), jnp.where(first_lane, m[1], im)
                    at = t * rows + g * SUB
                    out[pl.ds((odd * half + lanes) // LANES * tilts * rows + at, SUB), :] = re
                    out[pl.ds((odd * half + quarter + lanes) // LANES * tilts * rows + at, SUB), :] = im
    if out.shape[0] > sections * tilts * rows:
        tilt_of = lax.broadcasted_iota(jnp.int32, (tilts * count, 1), 0) % SUB // (SUB // tilts)
        dc = scaled[0, :, :1]
        sums = [jnp.sum(jnp.where(tilt_of == t, dc, 0.0), axis=0, keepdims=True) for t in range(tilts)]
        tail = jnp.concatenate(sums + [jnp.zeros((SUB - tilts, 1), F32)], axis=0)
        out[pl.ds(sections * tilts * rows, SUB), :] = jnp.broadcast_to(tail, (SUB, LANES))


def back_signal_kernel(first, spec, forms, local, lse, table, out, scaled, half_spectrum):
    back_project(first, spec, forms, local, lse, half_spectrum, scaled)
    rows = out.shape[0]
    sections = out.shape[1] // LANES
    parts = [half_spectrum[pl.ds(s * rows, rows), :] for s in range(sections)]
    even = jnp.concatenate(parts[: sections // 2], axis=1)
    odd = jnp.concatenate(parts[sections // 2 :], axis=1)
    out[...] = from_half_spectrum(even, odd, table)


def back_own_kernel(forms, local, lse, frames, table, out, counts, spec, scaled, sem):
    count, share, angles = spec.shape
    half = angles // 2
    copy = pltpu.make_async_copy(frames.at[:, pl.ds(own_shells(0, share), share), :], counts, sem)
    copy.start()
    copy.wait()
    chunk = min(count, 8)

    def step(c, carry):
        at = pl.ds(c * chunk, chunk)
        for odd, part in enumerate(spectra(counts[at], table)):
            spec[at, :, odd * half : (odd + 1) * half] = part
        return carry

    lax.fori_loop(0, count // chunk, step, 0)
    back_project(0, spec, forms, local, lse, out, scaled)


def back(shape, forms, local, lse, first, rows, spec=None, frames=None, table=None):
    count, share, angles = shape
    half = angles // 2
    tilts = forms.shape[1] // count
    vm = pl.BlockSpec(memory_space=pltpu.VMEM)
    scaled = pltpu.VMEM(forms.shape, F32)
    call = functools.partial(
        pl.pallas_call,
        out_shape=pltpu.VMEM((tilts * rows * (angles // LANES) + (0 if first else SUB), LANES), F32),
        out_specs=vm,
        compiler_params=pltpu.CompilerParams(vmem_limit_bytes=VMEM_BYTES),
        cost_estimate=pl.CostEstimate(
            flops=0 if spec is None else VECTOR_COST * 8 * count * tilts * rows * half,
            bytes_accessed=0 if spec is None else count * rows * angles * 4,
            transcendentals=0,
        ),
    )
    if spec is not None:
        if table is None:
            kernel = functools.partial(back_project, first)
            return call(kernel, in_specs=[vm] * 4, scratch_shapes=[scaled], name="back")(spec, forms, local, lse)
        return call(
            functools.partial(back_signal_kernel, first),
            out_shape=pltpu.VMEM((tilts * rows, angles), F32),
            in_specs=[vm] * 5,
            scratch_shapes=[scaled, pltpu.VMEM((tilts * rows * (angles // LANES), LANES), F32)],
            name="back_signal",
        )(spec, forms, local, lse, table)
    return call(
        back_own_kernel,
        in_specs=[vm] * 3 + [pl.BlockSpec(memory_space=pltpu.HBM), vm],
        scratch_shapes=[
            pltpu.VMEM(shape, jnp.int32),
            pltpu.VMEM(shape, F32),
            scaled,
            pltpu.SemaphoreType.DMA,
        ],
        name="back_own",
    )(forms, local, lse, in_hbm(frames), table)


def log_kernel(scores, lse, after, out):
    count, tilts, _ = out.shape
    chunk = SUB // tilts
    value = scores[...] - unpack_rows(lse[...], scores.shape[0] // SUB, tilts, scores.shape[1])
    for c in range(count // chunk):
        for t in range(tilts):
            at = c * SUB + t * chunk
            out[pl.ds(c * chunk, chunk), t, :] = value[at : at + chunk]


def update_kernel(own, other, slices, table, out, rest, factor, result, sem):
    tilts, rows, angles = result.shape
    share = out.shape[1]
    sections = angles // LANES

    def numer(first, count, extra):
        columns = []
        for s in range(sections):
            mine = [own[pl.ds((s * tilts + t) * share + first, count), :] for t in range(tilts)]
            column = jnp.concatenate(mine, axis=0)
            columns.append(column + extra[pl.ds(s * tilts * count, tilts * count), :] if extra is not None else column)
        even = jnp.concatenate(columns[: sections // 2], axis=1)
        odd = jnp.concatenate(columns[sections // 2 :], axis=1)
        return from_half_spectrum(even, odd, table)

    at = [ref[pl.ds(ref.shape[0] - SUB, SUB), :] for ref in (own, other)]
    scale = 1.0 / (at[0] + at[1] + 1.0)
    base = own_shells(0, share)
    done = numer(0, rows, other)
    for t in range(tilts):
        before = slices[t, pl.ds(base, rows), :]
        result[t] = (done[t * rows : (t + 1) * rows] + before) * scale[t : t + 1, :1]
    copy = pltpu.make_async_copy(result, out.at[:, pl.ds(0, rows), :], sem)
    copy.start()
    left = share - rows
    part = numer(rows, left, None)
    for t in range(tilts):
        to = slice(t * left, (t + 1) * left)
        before = slices[t, pl.ds(base + rows, left), :]
        rest[to, :] = (part[to] + before) * scale[t : t + 1, :1]
        factor[to, :] = jnp.broadcast_to(scale[t : t + 1, :], (left, LANES))
    copy.wait()


def finish_kernel(other, rest, factor, earlier, out, result, sem):
    tilts, rows, angles = result.shape
    share = out.shape[1]
    for lanes in range(0, angles, LANES):
        at = pl.ds(lanes, LANES)
        result[:, :, at] = (other[:, at] * factor[...] + rest[:, at]).reshape(tilts, rows, LANES)
    copy = pltpu.make_async_copy(result, out.at[:, pl.ds(share - rows, rows), :], sem)
    copy.start()
    copy.wait()


def update(own, others, slices, table, share, rows):
    tilts, _, angles = slices.shape
    left = share - rows
    hbm = pl.BlockSpec(memory_space=pltpu.HBM)
    vm = pl.BlockSpec(memory_space=pltpu.VMEM)
    params = pltpu.CompilerParams(vmem_limit_bytes=VMEM_BYTES)
    whole = jax.ShapeDtypeStruct((tilts, share, angles), F32)
    new, rest, factor = pl.pallas_call(
        update_kernel,
        out_shape=(whole, pltpu.VMEM((tilts * left, angles), F32), pltpu.VMEM((tilts * left, LANES), F32)),
        in_specs=[vm] * 4,
        out_specs=(hbm, vm, vm),
        scratch_shapes=[pltpu.VMEM((tilts, rows, angles), F32), pltpu.SemaphoreType.DMA],
        compiler_params=params,
        name="update",
    )(own, others[0], slices, table)
    return pl.pallas_call(
        finish_kernel,
        out_shape=whole,
        in_specs=[vm] * 3 + [hbm],
        out_specs=hbm,
        scratch_shapes=[pltpu.VMEM((tilts, left, angles), F32), pltpu.SemaphoreType.DMA],
        input_output_aliases={3: 0},
        compiler_params=params,
        name="finish",
    )(others[1], rest, factor, new)


def log_sum(values):
    top = functools.reduce(jnp.maximum, values)
    return top + jnp.log(sum(jnp.exp(value - top) for value in values))


def over_axis(value, axis):
    size = lax.axis_size(axis)
    if size & (size - 1):
        return jax.nn.logsumexp(lax.all_gather(value, axis), axis=0)
    bits = [1 << i for i in range(size.bit_length() - 1)]
    rounds = [[bit] for bit in bits[:1]] + [bits[i : i + 2] for i in range(1, len(bits), 2)]
    for bits in rounds:
        steps = [step | 1 for step in ([*bits, sum(bits)] if len(bits) == 2 else bits)]
        parts = [lax.ppermute(value, axis, [(i, i ^ step) for i in range(size)]) for step in steps]
        value = log_sum([value, *parts])
    return value


def on_device(frames, slices):
    count, shells, angles = frames.shape
    tilts = slices.shape[0]
    anneal = 4.0 / math.sqrt(shells * angles)
    groups = lax.axis_size("dp")
    share = shells // groups
    table = jnp.asarray(spectrum_tables(angles))
    vm = pl.BlockSpec(memory_space=pltpu.VMEM)
    params = pltpu.CompilerParams(vmem_limit_bytes=VMEM_BYTES)

    spec, scores, local, table = expect(frames, slices, table, anneal, groups)
    forms = pl.pallas_call(
        functools.partial(weights_kernel, tilts),
        out_shape=pltpu.VMEM((3, tilts * count, angles // 2), F32),
        in_specs=[vm] * 3,
        out_specs=vm,
        compiler_params=params,
        cost_estimate=pl.CostEstimate(flops=3 * tilts * count * angles * angles, bytes_accessed=2 * angles * angles, transcendentals=0),
        name="transform",
    )(scores, local, table)
    lse = over_axis(local, "rot")

    shape = (count, share, angles)
    rows = share // 2 // SUB * SUB
    others = []
    for first, shells_, signal in ((0, rows, None), (rows, share - rows, table)):
        got = None
        for step in range(1, groups):
            block = back(shape, forms, local, lse, first, shells_, spec=spec[step - 1], table=signal)
            block = lax.ppermute(block, "dp", [(i, (i + step) % groups) for i in range(groups)])
            got = block if got is None else got + block
        others.append(got)
    own = back(shape, forms, local, lse, 0, share, frames=frames, table=table)
    log_resp = pl.pallas_call(
        log_kernel,
        out_shape=jax.ShapeDtypeStruct((count, tilts, angles), F32),
        in_specs=[vm, vm, pl.BlockSpec(memory_space=pl.ANY)],
        out_specs=vm,
        compiler_params=params,
        name="log_resp",
    )(scores, lse, others[0])
    new_slices = update(own, others, slices, table, share, rows)
    return (log_resp, new_slices)


def solution(mesh):
    in_specs = (P("dp", None, None), P("rot", None, None))
    out_specs = (P("dp", "rot", None), P("rot", "dp", None))
    return jax.shard_map(on_device, mesh=mesh, in_specs=in_specs, out_specs=out_specs, check_vma=False)
```

```python
import functools
import math

import jax
import jax.numpy as jnp
import ml_dtypes
import numpy as np
from jax import lax
from jax.experimental import pallas as pl
from jax.experimental.pallas import tpu as pltpu
from jax.sharding import PartitionSpec as P

BF = jnp.bfloat16
F32 = jnp.float32
LANES = 128
SUB = 8
VMEM_BYTES = 24 * 1024 * 1024
OWN_LOADS = 4
VECTOR_COST = 128


def spectrum_tables(n):
    half, quarter = n // 2, n // 4
    index = np.arange(half)
    pieces = []
    for odd in (0, 1):
        theta = (np.outer(index, 2 * np.arange(quarter) + odd) % n) * (2.0 * np.pi / n)
        table = np.concatenate([np.cos(theta), -np.sin(theta)], axis=1)
        if not odd:
            table[:, quarter] = np.where(index % 2 == 0, 1.0, -1.0)
        table = table.astype(np.float32)
        head = table.astype(ml_dtypes.bfloat16)
        pieces += [head, (table - head.astype(np.float32)).astype(ml_dtypes.bfloat16)]
    return np.stack(pieces)


def split2(x):
    head = x.astype(BF)
    return head, (x - head.astype(F32)).astype(BF)


def mm(a, b):
    return jnp.dot(a, b, preferred_element_type=F32)


def mm_t(a, b):
    return lax.dot_general(a, b, (((1,), (1,)), ((), ())), preferred_element_type=F32)


def times_table(x, table, odd, product=mm):
    rows = x.shape[0]
    x0, x1 = split2(x)
    both = product(jnp.concatenate([x0, x1], axis=0), table[2 * odd])
    return both[:rows] + (both[rows:] + product(x0, table[2 * odd + 1]))


def fold(x):
    half = x.shape[-1] // 2
    low, high = x[..., :half], x[..., half:]
    return low + high, low - high


def to_half_spectrum(x, table):
    return [times_table(part, table, odd) for odd, part in enumerate(fold(x))]


def from_half_spectrum(even, odd, table):
    n = 2 * even.shape[1]
    lane = lax.broadcasted_iota(jnp.int32, even.shape, 1)
    weight = jnp.where((lane == 0) | (lane == n // 4), 1.0 / n, 2.0 / n)
    even = times_table(even * weight, table, 0, mm_t)
    odd = times_table(odd * (2.0 / n), table, 1, mm_t)
    return jnp.concatenate([even + odd, even - odd], axis=1)


def sublane_sums(parts):
    row = lax.broadcasted_iota(jnp.int32, parts[0].shape, 0)
    width = SUB // 2
    while width:
        low = (row & width) == 0
        merged = []
        for i in range(width):
            a, b = parts[i], parts[i + width]
            kept, moved = jnp.where(low, a, b), jnp.where(low, b, a)
            if 2 * width == SUB:
                moved = pltpu.roll(moved, width, 0)
            else:
                moved = jnp.where(low, pltpu.roll(moved, SUB - width, 0), pltpu.roll(moved, width, 0))
            merged.append(kept + moved)
        parts = merged
        width //= 2
    return parts[0]


def frame_lanes(groups, tilts, group):
    frames = SUB // tilts
    step = LANES // (groups * frames)
    lane = lax.broadcasted_iota(jnp.int32, (SUB, LANES), 1)
    row = lax.broadcasted_iota(jnp.int32, (SUB, LANES), 0)
    return lane, (group * frames + row % frames) * step, step


def pack_rows(x, tilts):
    groups = x.shape[0] // SUB
    row = lax.broadcasted_iota(jnp.int32, (SUB, LANES), 0)
    packed = jnp.zeros((SUB, LANES), F32)
    for i in range(groups):
        lane, first, step = frame_lanes(groups, tilts, i)
        here = (lane >= first) & (lane < first + step) & (row < SUB // tilts)
        packed = jnp.where(here, x[i * SUB : (i + 1) * SUB], packed)
    return jnp.sum(packed, axis=0, keepdims=True)


def unpack_rows(packed, groups, tilts, width):
    wide = jnp.broadcast_to(packed, (SUB, LANES))
    rows = []
    for i in range(groups):
        _, first, _ = frame_lanes(groups, tilts, i)
        row = jnp.take_along_axis(wide, first, axis=1, mode="promise_in_bounds")
        rows.append(jnp.concatenate([row] * (width // LANES), axis=1))
    return jnp.concatenate(rows, axis=0)


def lane_zero(shape):
    return lax.broadcasted_iota(jnp.int32, shape, len(shape) - 1) == 0


def even_forms(re, im):
    first = lane_zero(re.shape)
    return re, jnp.where(first, 0.0, im), jnp.where(first, im, re)


def spectra(counts, table):
    shape = counts.shape[:2]
    half = counts.shape[2] // 2
    return [
        mm(part.reshape(-1, half), table[2 * odd]).reshape(*shape, half)
        for odd, part in enumerate(fold(counts.astype(F32).astype(BF)))
    ]


def own_shells(step, share):
    groups = lax.axis_size("dp")
    return pl.multiple_of(lax.rem(lax.axis_index("dp") + step, groups) * share, SUB)


def expect_kernel(anneal, chunk, groups, frames, slices, table, *refs):
    count, shells, angles = frames.shape
    tilts = slices.shape[0]
    half, quarter = angles // 2, angles // 4
    chunks = count // chunk
    share = shells // groups
    rows = tilts * shells
    other, refs = refs[: groups - 1], refs[groups - 1 :]
    scores, local, tv, own, fbuf, sbuf, ya, yb, yc, cross, sems = refs
    spec = (own, *other)
    bases = [own_shells(s, share) for s in range(groups)]

    def frame_copy(c):
        at = pl.ds(c * chunk, chunk)
        return pltpu.make_async_copy(frames.at[at], fbuf.at[at], sems.at[2 + c])

    table_copy = pltpu.make_async_copy(table, tv, sems.at[0])
    slice_copy = pltpu.make_async_copy(slices, sbuf, sems.at[1])

    def transform(c):
        at = pl.ds(c * chunk, chunk)
        counts = jnp.concatenate([fbuf[at, pl.ds(base, share), :] for base in bases], axis=1)
        for odd, part in enumerate(spectra(counts, tv)):
            for s in range(groups):
                spec[s][at, :, odd * half : (odd + 1) * half] = part[:, s * share : (s + 1) * share]

    def correlate(c):
        out = pl.ds(c * SUB, SUB)
        for odd in range(2):
            for lanes in range(0, quarter, LANES):
                re_l = pl.ds(odd * half + lanes, LANES)
                im_l = pl.ds(odd * half + quarter + lanes, LANES)
                y_l = pl.ds(odd * quarter + lanes, LANES)
                sums = [[None] * SUB for _ in range(3)]
                for pair in range(0, chunk, 2):
                    for s in range(groups):
                        for g in range(share // SUB):
                            r = pl.ds(g * SUB, SUB)
                            ks = [c * chunk + pair + q for q in range(2)]
                            xs = [(spec[s][k, r, re_l], spec[s][k, r, im_l]) for k in ks]
                            xs = [(xr, xi, xr + xi) for xr, xi in xs]
                            for t in range(tilts):
                                y = pl.ds(bases[s] + (t * shells + g * SUB), SUB)
                                ys = ya[y, y_l], yb[y, y_l], yc[y, y_l]
                                for q in range(2):
                                    at = t * chunk + pair + q
                                    for i in range(3):
                                        u = xs[q][i] * ys[i]
                                        sums[i][at] = u if sums[i][at] is None else sums[i][at] + u
                m = [sublane_sums(part) for part in sums]
                re, im = m[0] + m[1], m[2] - m[0] + m[1]
                if lanes == 0 and not odd:
                    first = lane_zero(re.shape)
                    re, im = jnp.where(first, m[0], re), jnp.where(first, m[1], im)
                cross[out, re_l] = re
                cross[out, im_l] = im

    slice_copy.start()
    table_copy.start()
    for c in range(chunks):
        frame_copy(c).start()

    slice_copy.wait()
    logs = jnp.log(sbuf[...]).reshape(rows, angles)
    folded = fold(logs)
    dc = jnp.sum(logs, axis=1, keepdims=True)
    table_copy.wait()
    even, odd = [times_table(part, tv, i) for i, part in enumerate(folded)]
    even_re = jnp.where(lane_zero((rows, quarter)), dc, even[:, :quarter])
    for i, (re, im) in enumerate(((even_re, even[:, quarter:]), (odd[:, :quarter], odd[:, quarter:]))):
        at = slice(i * quarter, (i + 1) * quarter)
        ya[:, at] = re
        yb[:, at] = im
        yc[:, at] = re - im

    early = max(chunks - 2, 0)
    waits = {c: (c,) for c in range(early)} | {early: range(early, chunks)}
    for c in range(chunks):
        for later in waits.get(c, ()):
            frame_copy(later).wait()
        transform(c)
        if c < early:
            correlate(c)
    for c in range(early, chunks):
        correlate(c)

    spectrum = cross[...]
    dc = spectrum[:, :1]
    even = spectrum[:, :half]
    even = jnp.where(lane_zero(even.shape), 0.0, even)
    corr = from_half_spectrum(even, spectrum[:, half:], tv) + dc * (1.0 / angles)
    totals = [
        jnp.broadcast_to(jnp.sum(jnp.sum(sbuf[t], axis=0, keepdims=True), axis=1, keepdims=True), (chunk, 1))
        for t in range(tilts)
    ]
    part = anneal * (corr - jnp.concatenate(totals * chunks, axis=0))
    scores[...] = part

    def over_tilts(x, join):
        parts = []
        for c in range(chunks):
            group = x[c * SUB : (c + 1) * SUB]
            shift = chunk
            while shift < SUB:
                group = join(group, pltpu.roll(group, shift, 0))
                shift *= 2
            parts.append(group)
        return jnp.concatenate(parts, axis=0)

    wide = (tilts * count, LANES)
    top = over_tilts(jnp.broadcast_to(jnp.max(part, axis=1, keepdims=True), wide), jnp.maximum)
    total = jnp.sum(jnp.exp(part - top[:, :1]), axis=1, keepdims=True)
    local[...] = pack_rows(top + jnp.log(over_tilts(jnp.broadcast_to(total, wide), jnp.add)), tilts)


def in_hbm(x):
    return pltpu.with_memory_space_constraint(x, pltpu.HBM)


def expect(frames, slices, table, anneal, groups):
    count, shells, angles = frames.shape
    tilts = slices.shape[0]
    half = angles // 2
    chunk = SUB // tilts
    share = shells // groups
    hbm = pl.BlockSpec(memory_space=pltpu.HBM)
    vm = pl.BlockSpec(memory_space=pltpu.VMEM)
    form = pltpu.VMEM((tilts * shells, half), F32)
    *other, scores, local, table = pl.pallas_call(
        functools.partial(expect_kernel, anneal, chunk, groups),
        out_shape=(
            *[pltpu.VMEM((count, share, angles), F32)] * (groups - 1),
            pltpu.VMEM((tilts * count, angles), F32),
            pltpu.VMEM((1, LANES), F32),
            pltpu.VMEM(table.shape, BF),
        ),
        in_specs=[hbm] * 3,
        out_specs=(*[vm] * (groups - 1), vm, vm, vm),
        scratch_shapes=[
            pltpu.VMEM((count, share, angles), F32),
            pltpu.VMEM((count, shells, angles), jnp.int32),
            pltpu.VMEM((tilts, shells, angles), F32),
            form,
            form,
            form,
            pltpu.VMEM((tilts * count, angles), F32),
            pltpu.SemaphoreType.DMA((2 + count // chunk,)),
        ],
        compiler_params=pltpu.CompilerParams(vmem_limit_bytes=VMEM_BYTES),
        name="expect",
    )(*(in_hbm(x) for x in (frames, slices, table)))
    return other, scores, local, table


def weights_kernel(tilts, scores, local, table, forms):
    own = jnp.exp(scores[...] - unpack_rows(local[...], scores.shape[0] // SUB, tilts, scores.shape[1]))
    quarter = own.shape[1] // 4
    for odd, part in enumerate(to_half_spectrum(own, table)):
        re, im = part[:, :quarter], part[:, quarter:]
        at = slice(odd * quarter, (odd + 1) * quarter)
        forms[0, :, at] = re
        forms[1, :, at] = im
        forms[2, :, at] = re - im


def row_of(k, t, tilts):
    chunk = SUB // tilts
    return k // chunk * SUB + t * chunk + k % chunk


def back_project(first, spec, forms, local, lse, out, scaled):
    count, _, angles = spec.shape
    half, quarter = angles // 2, angles // 4
    sections = angles // LANES
    tilts = forms.shape[1] // count
    rows = out.shape[0] // SUB * SUB // sections // (SUB * tilts) * SUB
    factor = unpack_rows(jnp.exp(local[...] - lse[...]), tilts * count // SUB, tilts, half)
    scaled[...] = forms[...] * factor[None]
    for odd in range(2):
        for lanes in range(0, quarter, LANES):
            re_l = pl.ds(odd * half + lanes, LANES)
            im_l = pl.ds(odd * half + quarter + lanes, LANES)
            p_l = pl.ds(odd * quarter + lanes, LANES)
            for g in range(rows // SUB):
                r = pl.ds(first + g * SUB, SUB)
                sums = [[None] * tilts for _ in range(3)]
                for k in range(count):
                    xr, xi = spec[k, r, re_l], spec[k, r, im_l]
                    xs = xr, xi, xr + xi
                    for t in range(tilts):
                        row = pl.ds(row_of(k, t, tilts), 1)
                        for i in range(3):
                            u = xs[i] * scaled[i, row, p_l]
                            sums[i][t] = u if k == 0 else sums[i][t] + u
                for t in range(tilts):
                    m = [part[t] for part in sums]
                    re, im = m[0] + m[1], m[2] - m[0] + m[1]
                    if lanes == 0 and not odd:
                        first_lane = lane_zero(re.shape)
                        re, im = jnp.where(first_lane, m[0], re), jnp.where(first_lane, m[1], im)
                    at = t * rows + g * SUB
                    out[pl.ds((odd * half + lanes) // LANES * tilts * rows + at, SUB), :] = re
                    out[pl.ds((odd * half + quarter + lanes) // LANES * tilts * rows + at, SUB), :] = im
    if out.shape[0] > sections * tilts * rows:
        tilt_of = lax.broadcasted_iota(jnp.int32, (tilts * count, 1), 0) % SUB // (SUB // tilts)
        dc = scaled[0, :, :1]
        sums = [jnp.sum(jnp.where(tilt_of == t, dc, 0.0), axis=0, keepdims=True) for t in range(tilts)]
        tail = jnp.concatenate(sums + [jnp.zeros((SUB - tilts, 1), F32)], axis=0)
        out[pl.ds(sections * tilts * rows, SUB), :] = jnp.broadcast_to(tail, (SUB, LANES))


def back_signal_kernel(first, spec, forms, local, lse, table, out, scaled, half_spectrum):
    back_project(first, spec, forms, local, lse, half_spectrum, scaled)
    rows = out.shape[0]
    sections = out.shape[1] // LANES
    parts = [half_spectrum[pl.ds(s * rows, rows), :] for s in range(sections)]
    even = jnp.concatenate(parts[: sections // 2], axis=1)
    odd = jnp.concatenate(parts[sections // 2 :], axis=1)
    out[...] = from_half_spectrum(even, odd, table)


def back_own_kernel(forms, local, lse, frames, table, out, counts, spec, scaled, sem):
    count, share, angles = spec.shape
    half = angles // 2
    chunk = count // OWN_LOADS
    parts = [pl.ds(c * chunk, chunk) for c in range(OWN_LOADS)]
    copies = [
        pltpu.make_async_copy(frames.at[at, pl.ds(own_shells(0, share), share), :], counts.at[at], sem.at[c])
        for c, at in enumerate(parts)
    ]
    for copy in copies:
        copy.start()
    for at, copy in zip(parts, copies):
        copy.wait()
        for odd, part in enumerate(spectra(counts[at], table)):
            spec[at, :, odd * half : (odd + 1) * half] = part
    back_project(0, spec, forms, local, lse, out, scaled)


def back(shape, forms, local, lse, first, rows, spec=None, frames=None, table=None):
    count, share, angles = shape
    half = angles // 2
    tilts = forms.shape[1] // count
    vm = pl.BlockSpec(memory_space=pltpu.VMEM)
    scaled = pltpu.VMEM(forms.shape, F32)
    call = functools.partial(
        pl.pallas_call,
        out_shape=pltpu.VMEM((tilts * rows * (angles // LANES) + (0 if first else SUB), LANES), F32),
        out_specs=vm,
        compiler_params=pltpu.CompilerParams(vmem_limit_bytes=VMEM_BYTES),
        cost_estimate=pl.CostEstimate(
            flops=0 if spec is None else VECTOR_COST * 8 * count * tilts * rows * half,
            bytes_accessed=0 if spec is None else count * rows * angles * 4,
            transcendentals=0,
        ),
    )
    if spec is not None:
        if table is None:
            kernel = functools.partial(back_project, first)
            return call(kernel, in_specs=[vm] * 4, scratch_shapes=[scaled], name="back")(spec, forms, local, lse)
        return call(
            functools.partial(back_signal_kernel, first),
            out_shape=pltpu.VMEM((tilts * rows, angles), F32),
            in_specs=[vm] * 5,
            scratch_shapes=[scaled, pltpu.VMEM((tilts * rows * (angles // LANES), LANES), F32)],
            name="back_signal",
        )(spec, forms, local, lse, table)
    return call(
        back_own_kernel,
        in_specs=[vm] * 3 + [pl.BlockSpec(memory_space=pltpu.HBM), vm],
        scratch_shapes=[
            pltpu.VMEM(shape, jnp.int32),
            pltpu.VMEM(shape, F32),
            scaled,
            pltpu.SemaphoreType.DMA((OWN_LOADS,)),
        ],
        name="back_own",
    )(forms, local, lse, in_hbm(frames), table)


def log_responsibilities(scores, lse, out):
    count, tilts, _ = out.shape
    chunk = SUB // tilts
    value = scores[...] - unpack_rows(lse[...], scores.shape[0] // SUB, tilts, scores.shape[1])
    for c in range(count // chunk):
        for t in range(tilts):
            at = c * SUB + t * chunk
            out[pl.ds(c * chunk, chunk), t, :] = value[at : at + chunk]


def update_kernel(own, other, slices, table, scores, lse, out, logs, rest, factor, result, value, sem, log_sem):
    tilts, rows, angles = result.shape
    share = out.shape[1]
    sections = angles // LANES
    log_responsibilities(scores, lse, value)
    log_copy = pltpu.make_async_copy(value, logs, log_sem)
    log_copy.start()

    def numer(first, count, extra):
        columns = []
        for s in range(sections):
            mine = [own[pl.ds((s * tilts + t) * share + first, count), :] for t in range(tilts)]
            column = jnp.concatenate(mine, axis=0)
            columns.append(column + extra[pl.ds(s * tilts * count, tilts * count), :] if extra is not None else column)
        even = jnp.concatenate(columns[: sections // 2], axis=1)
        odd = jnp.concatenate(columns[sections // 2 :], axis=1)
        return from_half_spectrum(even, odd, table)

    at = [ref[pl.ds(ref.shape[0] - SUB, SUB), :] for ref in (own, other)]
    scale = 1.0 / (at[0] + at[1] + 1.0)
    base = own_shells(0, share)
    done = numer(0, rows, other)
    for t in range(tilts):
        before = slices[t, pl.ds(base, rows), :]
        result[t] = (done[t * rows : (t + 1) * rows] + before) * scale[t : t + 1, :1]
    copy = pltpu.make_async_copy(result, out.at[:, pl.ds(0, rows), :], sem)
    copy.start()
    left = share - rows
    part = numer(rows, left, None)
    for t in range(tilts):
        to = slice(t * left, (t + 1) * left)
        before = slices[t, pl.ds(base + rows, left), :]
        rest[to, :] = (part[to] + before) * scale[t : t + 1, :1]
        factor[to, :] = jnp.broadcast_to(scale[t : t + 1, :], (left, LANES))
    copy.wait()
    log_copy.wait()


def finish_kernel(*refs):
    *others, rest, factor, earlier, out, result, sem = refs
    tilts, left, angles = result.shape
    share = out.shape[1]
    first = 0
    for other in others:
        rows = other.shape[0] // tilts
        for t in range(tilts):
            at = pl.ds(t * left + first, rows)
            scale = jnp.concatenate([factor[at, :]] * (angles // LANES), axis=1)
            result[t, pl.ds(first, rows), :] = other[pl.ds(t * rows, rows), :] * scale + rest[at, :]
        first += rows
    copy = pltpu.make_async_copy(result, out.at[:, pl.ds(share - left, left), :], sem)
    copy.start()
    copy.wait()


def update(own, others, slices, table, scores, lse, share, rows):
    tilts, _, angles = slices.shape
    left = share - rows
    hbm = pl.BlockSpec(memory_space=pltpu.HBM)
    vm = pl.BlockSpec(memory_space=pltpu.VMEM)
    params = pltpu.CompilerParams(vmem_limit_bytes=VMEM_BYTES)
    whole = jax.ShapeDtypeStruct((tilts, share, angles), F32)
    log_shape = (scores.shape[0] // tilts, tilts, angles)
    new, log_resp, rest, factor = pl.pallas_call(
        update_kernel,
        out_shape=(
            whole,
            jax.ShapeDtypeStruct(log_shape, F32),
            pltpu.VMEM((tilts * left, angles), F32),
            pltpu.VMEM((tilts * left, LANES), F32),
        ),
        in_specs=[vm] * 6,
        out_specs=(hbm, hbm, vm, vm),
        scratch_shapes=[
            pltpu.VMEM((tilts, rows, angles), F32),
            pltpu.VMEM(log_shape, F32),
            pltpu.SemaphoreType.DMA,
            pltpu.SemaphoreType.DMA,
        ],
        compiler_params=params,
        name="update",
    )(own, others[0], slices, table, scores, lse)
    new = pl.pallas_call(
        finish_kernel,
        out_shape=whole,
        in_specs=[vm] * (len(others) + 1) + [hbm],
        out_specs=hbm,
        scratch_shapes=[pltpu.VMEM((tilts, left, angles), F32), pltpu.SemaphoreType.DMA],
        input_output_aliases={len(others) + 1: 0},
        compiler_params=params,
        name="finish",
    )(*others[1:], rest, factor, new)
    return log_resp, new


def log_sum(values):
    top = functools.reduce(jnp.maximum, values)
    return top + jnp.log(sum(jnp.exp(value - top) for value in values))


def over_axis(value, axis):
    size = lax.axis_size(axis)
    if size & (size - 1):
        return jax.nn.logsumexp(lax.all_gather(value, axis), axis=0)
    bits = [1 << i for i in range(size.bit_length() - 1)]
    rounds = [[bit] for bit in bits[:1]] + [bits[i : i + 2] for i in range(1, len(bits), 2)]
    for bits in rounds:
        steps = [step | 1 for step in ([*bits, sum(bits)] if len(bits) == 2 else bits)]
        parts = [lax.ppermute(value, axis, [(i, i ^ step) for i in range(size)]) for step in steps]
        value = log_sum([value, *parts])
    return value


def on_device(frames, slices):
    count, shells, angles = frames.shape
    tilts = slices.shape[0]
    anneal = 4.0 / math.sqrt(shells * angles)
    groups = lax.axis_size("dp")
    share = shells // groups
    table = jnp.asarray(spectrum_tables(angles))
    vm = pl.BlockSpec(memory_space=pltpu.VMEM)
    params = pltpu.CompilerParams(vmem_limit_bytes=VMEM_BYTES)

    spec, scores, local, table = expect(frames, slices, table, anneal, groups)
    forms = pl.pallas_call(
        functools.partial(weights_kernel, tilts),
        out_shape=pltpu.VMEM((3, tilts * count, angles // 2), F32),
        in_specs=[vm] * 3,
        out_specs=vm,
        compiler_params=params,
        cost_estimate=pl.CostEstimate(flops=3 * tilts * count * angles * angles, bytes_accessed=2 * angles * angles, transcendentals=0),
        name="transform",
    )(scores, local, table)
    lse = over_axis(local, "rot")

    shape = (count, share, angles)
    units = share // SUB
    rows = max(3 * units // 8, 1) * SUB
    others = []
    for first in range(0, share, rows):
        shells_, signal = min(rows, share - first), table if first else None
        got = None
        for step in range(1, groups):
            block = back(shape, forms, local, lse, first, shells_, spec=spec[step - 1], table=signal)
            block = lax.ppermute(block, "dp", [(i, (i + step) % groups) for i in range(groups)])
            got = block if got is None else got + block
        others.append(got)
    own = back(shape, forms, local, lse, 0, share, frames=frames, table=table)
    return update(own, others, slices, table, scores, lse, share, rows)


def solution(mesh):
    in_specs = (P("dp", None, None), P("rot", None, None))
    out_specs = (P("dp", "rot", None), P("rot", "dp", None))
    return jax.shard_map(on_device, mesh=mesh, in_specs=in_specs, out_specs=out_specs, check_vma=False)
```

```python
import functools
import math

import jax
import jax.numpy as jnp
import ml_dtypes
import numpy as np
from jax import lax
from jax.experimental import pallas as pl
from jax.experimental.pallas import tpu as pltpu
from jax.sharding import PartitionSpec as P

BF = jnp.bfloat16
F32 = jnp.float32
LANES = 128
SUB = 8
VMEM_BYTES = 24 * 1024 * 1024
OWN_LOADS = 4
VECTOR_COST = 128


def spectrum_tables(n):
    half, quarter = n // 2, n // 4
    index = np.arange(half)
    pieces = []
    for odd in (0, 1):
        theta = (np.outer(index, 2 * np.arange(quarter) + odd) % n) * (2.0 * np.pi / n)
        table = np.concatenate([np.cos(theta), -np.sin(theta)], axis=1)
        if not odd:
            table[:, quarter] = np.where(index % 2 == 0, 1.0, -1.0)
        table = table.astype(np.float32)
        head = table.astype(ml_dtypes.bfloat16)
        pieces += [head, (table - head.astype(np.float32)).astype(ml_dtypes.bfloat16)]
    return np.stack(pieces)


def split2(x):
    head = x.astype(BF)
    return head, (x - head.astype(F32)).astype(BF)


def mm(a, b):
    return jnp.dot(a, b, preferred_element_type=F32)


def mm_t(a, b):
    return lax.dot_general(a, b, (((1,), (1,)), ((), ())), preferred_element_type=F32)


def times_table(x, table, odd, product=mm):
    rows = x.shape[0]
    x0, x1 = split2(x)
    both = product(jnp.concatenate([x0, x1], axis=0), table[2 * odd])
    return both[:rows] + (both[rows:] + product(x0, table[2 * odd + 1]))


def fold(x):
    half = x.shape[-1] // 2
    low, high = x[..., :half], x[..., half:]
    return low + high, low - high


def to_half_spectrum(x, table):
    return [times_table(part, table, odd) for odd, part in enumerate(fold(x))]


def from_half_spectrum(even, odd, table):
    n = 2 * even.shape[1]
    lane = lax.broadcasted_iota(jnp.int32, even.shape, 1)
    weight = jnp.where((lane == 0) | (lane == n // 4), 1.0 / n, 2.0 / n)
    even = times_table(even * weight, table, 0, mm_t)
    odd = times_table(odd * (2.0 / n), table, 1, mm_t)
    return jnp.concatenate([even + odd, even - odd], axis=1)


def sublane_sums(parts):
    row = lax.broadcasted_iota(jnp.int32, parts[0].shape, 0)
    width = SUB // 2
    while width:
        low = (row & width) == 0
        merged = []
        for i in range(width):
            a, b = parts[i], parts[i + width]
            kept, moved = jnp.where(low, a, b), jnp.where(low, b, a)
            if 2 * width == SUB:
                moved = pltpu.roll(moved, width, 0)
            else:
                moved = jnp.where(low, pltpu.roll(moved, SUB - width, 0), pltpu.roll(moved, width, 0))
            merged.append(kept + moved)
        parts = merged
        width //= 2
    return parts[0]


def frame_lanes(groups, tilts, group):
    frames = SUB // tilts
    step = LANES // (groups * frames)
    lane = lax.broadcasted_iota(jnp.int32, (SUB, LANES), 1)
    row = lax.broadcasted_iota(jnp.int32, (SUB, LANES), 0)
    return lane, (group * frames + row % frames) * step, step


def pack_rows(x, tilts):
    groups = x.shape[0] // SUB
    row = lax.broadcasted_iota(jnp.int32, (SUB, LANES), 0)
    packed = jnp.zeros((SUB, LANES), F32)
    for i in range(groups):
        lane, first, step = frame_lanes(groups, tilts, i)
        here = (lane >= first) & (lane < first + step) & (row < SUB // tilts)
        packed = jnp.where(here, x[i * SUB : (i + 1) * SUB], packed)
    return jnp.sum(packed, axis=0, keepdims=True)


def unpack_rows(packed, groups, tilts, width):
    wide = jnp.broadcast_to(packed, (SUB, LANES))
    rows = []
    for i in range(groups):
        _, first, _ = frame_lanes(groups, tilts, i)
        row = jnp.take_along_axis(wide, first, axis=1, mode="promise_in_bounds")
        rows.append(jnp.concatenate([row] * (width // LANES), axis=1))
    return jnp.concatenate(rows, axis=0)


def lane_zero(shape):
    return lax.broadcasted_iota(jnp.int32, shape, len(shape) - 1) == 0


def even_forms(re, im):
    first = lane_zero(re.shape)
    return re, jnp.where(first, 0.0, im), jnp.where(first, im, re)


def spectra(counts, table):
    shape = counts.shape[:2]
    half = counts.shape[2] // 2
    return [
        mm(part.reshape(-1, half), table[2 * odd]).reshape(*shape, half)
        for odd, part in enumerate(fold(counts.astype(F32).astype(BF)))
    ]


def own_shells(step, share):
    groups = lax.axis_size("dp")
    return pl.multiple_of(lax.rem(lax.axis_index("dp") + step, groups) * share, SUB)


def expect_kernel(anneal, chunk, groups, frames, slices, table, *refs):
    count, shells, angles = frames.shape
    tilts = slices.shape[0]
    half, quarter = angles // 2, angles // 4
    chunks = count // chunk
    share = shells // groups
    rows = tilts * shells
    other, refs = refs[: groups - 1], refs[groups - 1 :]
    scores, local, tv, own, fbuf, sbuf, ya, yb, yc, cross, sems = refs
    spec = (own, *other)
    bases = [own_shells(s, share) for s in range(groups)]

    def frame_copy(c):
        at = pl.ds(c * chunk, chunk)
        return pltpu.make_async_copy(frames.at[at], fbuf.at[at], sems.at[2 + c])

    table_copy = pltpu.make_async_copy(table, tv, sems.at[0])
    slice_copy = pltpu.make_async_copy(slices, sbuf, sems.at[1])

    def transform(c):
        at = pl.ds(c * chunk, chunk)
        counts = jnp.concatenate([fbuf[at, pl.ds(base, share), :] for base in bases], axis=1)
        for odd, part in enumerate(spectra(counts, tv)):
            for s in range(groups):
                spec[s][at, :, odd * half : (odd + 1) * half] = part[:, s * share : (s + 1) * share]

    def correlate(c):
        out = pl.ds(c * SUB, SUB)
        for odd in range(2):
            for lanes in range(0, quarter, LANES):
                re_l = pl.ds(odd * half + lanes, LANES)
                im_l = pl.ds(odd * half + quarter + lanes, LANES)
                y_l = pl.ds(odd * quarter + lanes, LANES)
                sums = [[None] * SUB for _ in range(3)]
                for pair in range(0, chunk, 2):
                    for s in range(groups):
                        for g in range(share // SUB):
                            r = pl.ds(g * SUB, SUB)
                            ks = [c * chunk + pair + q for q in range(2)]
                            xs = [(spec[s][k, r, re_l], spec[s][k, r, im_l]) for k in ks]
                            xs = [(xr, xi, xr + xi) for xr, xi in xs]
                            for t in range(tilts):
                                y = pl.ds(bases[s] + (t * shells + g * SUB), SUB)
                                ys = ya[y, y_l], yb[y, y_l], yc[y, y_l]
                                for q in range(2):
                                    at = t * chunk + pair + q
                                    for i in range(3):
                                        u = xs[q][i] * ys[i]
                                        sums[i][at] = u if sums[i][at] is None else sums[i][at] + u
                m = [sublane_sums(part) for part in sums]
                re, im = m[0] + m[1], m[2] - m[0] + m[1]
                if lanes == 0 and not odd:
                    first = lane_zero(re.shape)
                    re, im = jnp.where(first, m[0], re), jnp.where(first, m[1], im)
                cross[out, re_l] = re
                cross[out, im_l] = im

    slice_copy.start()
    table_copy.start()
    for c in range(chunks):
        frame_copy(c).start()

    slice_copy.wait()
    logs = jnp.log(sbuf[...]).reshape(rows, angles)
    folded = fold(logs)
    dc = jnp.sum(logs, axis=1, keepdims=True)
    table_copy.wait()
    even, odd = [times_table(part, tv, i) for i, part in enumerate(folded)]
    even_re = jnp.where(lane_zero((rows, quarter)), dc, even[:, :quarter])
    for i, (re, im) in enumerate(((even_re, even[:, quarter:]), (odd[:, :quarter], odd[:, quarter:]))):
        at = slice(i * quarter, (i + 1) * quarter)
        ya[:, at] = re
        yb[:, at] = im
        yc[:, at] = re - im

    early = max(chunks - 2, 0)
    waits = {c: (c,) for c in range(early)} | {early: range(early, chunks)}
    for c in range(chunks):
        for later in waits.get(c, ()):
            frame_copy(later).wait()
        transform(c)
        if c < early:
            correlate(c)
    for c in range(early, chunks):
        correlate(c)

    spectrum = cross[...]
    dc = spectrum[:, :1]
    even = spectrum[:, :half]
    even = jnp.where(lane_zero(even.shape), 0.0, even)
    corr = from_half_spectrum(even, spectrum[:, half:], tv) + dc * (1.0 / angles)
    totals = [
        jnp.broadcast_to(jnp.sum(jnp.sum(sbuf[t], axis=0, keepdims=True), axis=1, keepdims=True), (chunk, 1))
        for t in range(tilts)
    ]
    part = anneal * (corr - jnp.concatenate(totals * chunks, axis=0))
    scores[...] = part

    def over_tilts(x, join):
        parts = []
        for c in range(chunks):
            group = x[c * SUB : (c + 1) * SUB]
            shift = chunk
            while shift < SUB:
                group = join(group, pltpu.roll(group, shift, 0))
                shift *= 2
            parts.append(group)
        return jnp.concatenate(parts, axis=0)

    wide = (tilts * count, LANES)
    top = over_tilts(jnp.broadcast_to(jnp.max(part, axis=1, keepdims=True), wide), jnp.maximum)
    total = jnp.sum(jnp.exp(part - top[:, :1]), axis=1, keepdims=True)
    local[...] = pack_rows(top + jnp.log(over_tilts(jnp.broadcast_to(total, wide), jnp.add)), tilts)


def in_hbm(x):
    return pltpu.with_memory_space_constraint(x, pltpu.HBM)


def expect(frames, slices, table, anneal, groups):
    count, shells, angles = frames.shape
    tilts = slices.shape[0]
    half = angles // 2
    chunk = SUB // tilts
    share = shells // groups
    hbm = pl.BlockSpec(memory_space=pltpu.HBM)
    vm = pl.BlockSpec(memory_space=pltpu.VMEM)
    form = pltpu.VMEM((tilts * shells, half), F32)
    *other, scores, local, table = pl.pallas_call(
        functools.partial(expect_kernel, anneal, chunk, groups),
        out_shape=(
            *[pltpu.VMEM((count, share, angles), F32)] * (groups - 1),
            pltpu.VMEM((tilts * count, angles), F32),
            pltpu.VMEM((1, LANES), F32),
            pltpu.VMEM(table.shape, BF),
        ),
        in_specs=[hbm] * 3,
        out_specs=(*[vm] * (groups - 1), vm, vm, vm),
        scratch_shapes=[
            pltpu.VMEM((count, share, angles), F32),
            pltpu.VMEM((count, shells, angles), jnp.int32),
            pltpu.VMEM((tilts, shells, angles), F32),
            form,
            form,
            form,
            pltpu.VMEM((tilts * count, angles), F32),
            pltpu.SemaphoreType.DMA((2 + count // chunk,)),
        ],
        compiler_params=pltpu.CompilerParams(vmem_limit_bytes=VMEM_BYTES),
        name="expect",
    )(*(in_hbm(x) for x in (frames, slices, table)))
    return other, scores, local, table


def weights_kernel(tilts, scores, local, table, forms):
    own = jnp.exp(scores[...] - unpack_rows(local[...], scores.shape[0] // SUB, tilts, scores.shape[1]))
    quarter = own.shape[1] // 4
    for odd, part in enumerate(to_half_spectrum(own, table)):
        re, im = part[:, :quarter], part[:, quarter:]
        at = slice(odd * quarter, (odd + 1) * quarter)
        forms[0, :, at] = re
        forms[1, :, at] = im
        forms[2, :, at] = re - im


def row_of(k, t, tilts):
    chunk = SUB // tilts
    return k // chunk * SUB + t * chunk + k % chunk


def back_project(first, spec, forms, local, lse, out, scaled):
    count, _, angles = spec.shape
    half, quarter = angles // 2, angles // 4
    sections = angles // LANES
    tilts = forms.shape[1] // count
    rows = out.shape[0] // SUB * SUB // sections // (SUB * tilts) * SUB
    factor = unpack_rows(jnp.exp(local[...] - lse[...]), tilts * count // SUB, tilts, half)
    scaled[...] = forms[...] * factor[None]
    for odd in range(2):
        for lanes in range(0, quarter, LANES):
            re_l = pl.ds(odd * half + lanes, LANES)
            im_l = pl.ds(odd * half + quarter + lanes, LANES)
            p_l = pl.ds(odd * quarter + lanes, LANES)
            for g in range(rows // SUB):
                r = pl.ds(first + g * SUB, SUB)
                sums = [[None] * tilts for _ in range(3)]
                for k in range(count):
                    xr, xi = spec[k, r, re_l], spec[k, r, im_l]
                    xs = xr, xi, xr + xi
                    for t in range(tilts):
                        row = pl.ds(row_of(k, t, tilts), 1)
                        for i in range(3):
                            u = xs[i] * scaled[i, row, p_l]
                            sums[i][t] = u if k == 0 else sums[i][t] + u
                for t in range(tilts):
                    m = [part[t] for part in sums]
                    re, im = m[0] + m[1], m[2] - m[0] + m[1]
                    if lanes == 0 and not odd:
                        first_lane = lane_zero(re.shape)
                        re, im = jnp.where(first_lane, m[0], re), jnp.where(first_lane, m[1], im)
                    at = t * rows + g * SUB
                    out[pl.ds((odd * half + lanes) // LANES * tilts * rows + at, SUB), :] = re
                    out[pl.ds((odd * half + quarter + lanes) // LANES * tilts * rows + at, SUB), :] = im
    if out.shape[0] > sections * tilts * rows:
        tilt_of = lax.broadcasted_iota(jnp.int32, (tilts * count, 1), 0) % SUB // (SUB // tilts)
        dc = scaled[0, :, :1]
        sums = [jnp.sum(jnp.where(tilt_of == t, dc, 0.0), axis=0, keepdims=True) for t in range(tilts)]
        tail = jnp.concatenate(sums + [jnp.zeros((SUB - tilts, 1), F32)], axis=0)
        out[pl.ds(sections * tilts * rows, SUB), :] = jnp.broadcast_to(tail, (SUB, LANES))


def back_signal_kernel(first, spec, forms, local, lse, table, out, scaled, half_spectrum):
    back_project(first, spec, forms, local, lse, half_spectrum, scaled)
    rows = out.shape[0]
    sections = out.shape[1] // LANES
    parts = [half_spectrum[pl.ds(s * rows, rows), :] for s in range(sections)]
    even = jnp.concatenate(parts[: sections // 2], axis=1)
    odd = jnp.concatenate(parts[sections // 2 :], axis=1)
    out[...] = from_half_spectrum(even, odd, table)


def back_own_kernel(forms, local, lse, frames, table, out, counts, spec, scaled, sem):
    count, share, angles = spec.shape
    half = angles // 2
    chunk = count // OWN_LOADS
    parts = [pl.ds(c * chunk, chunk) for c in range(OWN_LOADS)]
    copies = [
        pltpu.make_async_copy(frames.at[at, pl.ds(own_shells(0, share), share), :], counts.at[at], sem.at[c])
        for c, at in enumerate(parts)
    ]
    for copy in copies:
        copy.start()
    for at, copy in zip(parts, copies):
        copy.wait()
        for odd, part in enumerate(spectra(counts[at], table)):
            spec[at, :, odd * half : (odd + 1) * half] = part
    back_project(0, spec, forms, local, lse, out, scaled)


def back(shape, forms, local, lse, first, rows, spec=None, frames=None, table=None):
    count, share, angles = shape
    half = angles // 2
    tilts = forms.shape[1] // count
    vm = pl.BlockSpec(memory_space=pltpu.VMEM)
    scaled = pltpu.VMEM(forms.shape, F32)
    call = functools.partial(
        pl.pallas_call,
        out_shape=pltpu.VMEM((tilts * rows * (angles // LANES) + (0 if first else SUB), LANES), F32),
        out_specs=vm,
        compiler_params=pltpu.CompilerParams(vmem_limit_bytes=VMEM_BYTES),
        cost_estimate=pl.CostEstimate(
            flops=0 if spec is None else VECTOR_COST * 8 * count * tilts * rows * half,
            bytes_accessed=0 if spec is None else count * rows * angles * 4,
            transcendentals=0,
        ),
    )
    if spec is not None:
        if table is None:
            kernel = functools.partial(back_project, first)
            return call(kernel, in_specs=[vm] * 4, scratch_shapes=[scaled], name="back")(spec, forms, local, lse)
        return call(
            functools.partial(back_signal_kernel, first),
            out_shape=pltpu.VMEM((tilts * rows, angles), F32),
            in_specs=[vm] * 5,
            scratch_shapes=[scaled, pltpu.VMEM((tilts * rows * (angles // LANES), LANES), F32)],
            name="back_signal",
        )(spec, forms, local, lse, table)
    return call(
        back_own_kernel,
        in_specs=[vm] * 3 + [pl.BlockSpec(memory_space=pltpu.HBM), vm],
        scratch_shapes=[
            pltpu.VMEM(shape, jnp.int32),
            pltpu.VMEM(shape, F32),
            scaled,
            pltpu.SemaphoreType.DMA((OWN_LOADS,)),
        ],
        name="back_own",
    )(forms, local, lse, in_hbm(frames), table)


def log_responsibilities(scores, lse, out):
    count, tilts, _ = out.shape
    chunk = SUB // tilts
    value = scores[...] - unpack_rows(lse[...], scores.shape[0] // SUB, tilts, scores.shape[1])
    for c in range(count // chunk):
        for t in range(tilts):
            at = c * SUB + t * chunk
            out[pl.ds(c * chunk, chunk), t, :] = value[at : at + chunk]


def update_kernel(own, other, slices, table, scores, lse, out, logs, rest, factor, result, value, sem, log_sem):
    tilts, rows, angles = result.shape
    share = out.shape[1]
    sections = angles // LANES
    log_responsibilities(scores, lse, value)
    log_copy = pltpu.make_async_copy(value, logs, log_sem)
    log_copy.start()

    def numer(first, count, extra):
        columns = []
        for s in range(sections):
            mine = [own[pl.ds((s * tilts + t) * share + first, count), :] for t in range(tilts)]
            column = jnp.concatenate(mine, axis=0)
            columns.append(column + extra[pl.ds(s * tilts * count, tilts * count), :] if extra is not None else column)
        even = jnp.concatenate(columns[: sections // 2], axis=1)
        odd = jnp.concatenate(columns[sections // 2 :], axis=1)
        return from_half_spectrum(even, odd, table)

    at = [ref[pl.ds(ref.shape[0] - SUB, SUB), :] for ref in (own, other)]
    scale = 1.0 / (at[0] + at[1] + 1.0)
    base = own_shells(0, share)
    done = numer(0, rows, other)
    for t in range(tilts):
        before = slices[t, pl.ds(base, rows), :]
        result[t] = (done[t * rows : (t + 1) * rows] + before) * scale[t : t + 1, :1]
    copy = pltpu.make_async_copy(result, out.at[:, pl.ds(0, rows), :], sem)
    copy.start()
    left = share - rows
    part = numer(rows, left, None)
    for t in range(tilts):
        to = slice(t * left, (t + 1) * left)
        before = slices[t, pl.ds(base + rows, left), :]
        rest[to, :] = (part[to] + before) * scale[t : t + 1, :1]
        factor[to, :] = jnp.broadcast_to(scale[t : t + 1, :], (left, LANES))
    copy.wait()
    log_copy.wait()


def finish_kernel(*refs):
    *others, rest, factor, earlier, out, result, sem = refs
    tilts, left, angles = result.shape
    share = out.shape[1]
    first = 0
    for other in others:
        rows = other.shape[0] // tilts
        for t in range(tilts):
            at = pl.ds(t * left + first, rows)
            scale = jnp.concatenate([factor[at, :]] * (angles // LANES), axis=1)
            result[t, pl.ds(first, rows), :] = other[pl.ds(t * rows, rows), :] * scale + rest[at, :]
        first += rows
    copy = pltpu.make_async_copy(result, out.at[:, pl.ds(share - left, left), :], sem)
    copy.start()
    copy.wait()


def update(own, others, slices, table, scores, lse, share, rows):
    tilts, _, angles = slices.shape
    left = share - rows
    hbm = pl.BlockSpec(memory_space=pltpu.HBM)
    vm = pl.BlockSpec(memory_space=pltpu.VMEM)
    params = pltpu.CompilerParams(vmem_limit_bytes=VMEM_BYTES)
    whole = jax.ShapeDtypeStruct((tilts, share, angles), F32)
    log_shape = (scores.shape[0] // tilts, tilts, angles)
    new, log_resp, rest, factor = pl.pallas_call(
        update_kernel,
        out_shape=(
            whole,
            jax.ShapeDtypeStruct(log_shape, F32),
            pltpu.VMEM((tilts * left, angles), F32),
            pltpu.VMEM((tilts * left, LANES), F32),
        ),
        in_specs=[vm] * 6,
        out_specs=(hbm, hbm, vm, vm),
        scratch_shapes=[
            pltpu.VMEM((tilts, rows, angles), F32),
            pltpu.VMEM(log_shape, F32),
            pltpu.SemaphoreType.DMA,
            pltpu.SemaphoreType.DMA,
        ],
        compiler_params=params,
        name="update",
    )(own, others[0], slices, table, scores, lse)
    new = pl.pallas_call(
        finish_kernel,
        out_shape=whole,
        in_specs=[vm] * (len(others) + 1) + [hbm],
        out_specs=hbm,
        scratch_shapes=[pltpu.VMEM((tilts, left, angles), F32), pltpu.SemaphoreType.DMA],
        input_output_aliases={len(others) + 1: 0},
        compiler_params=params,
        name="finish",
    )(*others[1:], rest, factor, new)
    return log_resp, new


def log_sum(values):
    top = functools.reduce(jnp.maximum, values)
    return top + jnp.log(sum(jnp.exp(value - top) for value in values))


def over_axis(value, axis):
    size = lax.axis_size(axis)
    if size & (size - 1):
        return jax.nn.logsumexp(lax.all_gather(value, axis), axis=0)
    bits = [1 << i for i in range(size.bit_length() - 1)]
    rounds = [[bit] for bit in bits[:1]] + [bits[i : i + 2] for i in range(1, len(bits), 2)]
    for bits in rounds:
        steps = [step | 1 for step in bits] + ([sum(bits)] if len(bits) == 2 else [])
        parts = [lax.ppermute(value, axis, [(i, i ^ step) for i in range(size)]) for step in steps]
        value = log_sum([value, *parts])
    return value


def on_device(frames, slices):
    count, shells, angles = frames.shape
    tilts = slices.shape[0]
    anneal = 4.0 / math.sqrt(shells * angles)
    groups = lax.axis_size("dp")
    share = shells // groups
    table = jnp.asarray(spectrum_tables(angles))
    vm = pl.BlockSpec(memory_space=pltpu.VMEM)
    params = pltpu.CompilerParams(vmem_limit_bytes=VMEM_BYTES)

    spec, scores, local, table = expect(frames, slices, table, anneal, groups)
    forms = pl.pallas_call(
        functools.partial(weights_kernel, tilts),
        out_shape=pltpu.VMEM((3, tilts * count, angles // 2), F32),
        in_specs=[vm] * 3,
        out_specs=vm,
        compiler_params=params,
        cost_estimate=pl.CostEstimate(flops=3 * tilts * count * angles * angles, bytes_accessed=2 * angles * angles, transcendentals=0),
        name="transform",
    )(scores, local, table)
    lse = over_axis(local, "rot")

    shape = (count, share, angles)
    units = share // SUB
    rows = max(3 * units // 8, 1) * SUB
    others = []
    for first in range(0, share, rows):
        shells_, signal = min(rows, share - first), table if first else None
        got = None
        for step in range(1, groups):
            block = back(shape, forms, local, lse, first, shells_, spec=spec[step - 1], table=signal)
            block = lax.ppermute(block, "dp", [(i, (i + step) % groups) for i in range(groups)])
            got = block if got is None else got + block
        others.append(got)
    own = back(shape, forms, local, lse, 0, share, frames=frames, table=table)
    return update(own, others, slices, table, scores, lse, share, rows)


def solution(mesh):
    in_specs = (P("dp", None, None), P("rot", None, None))
    out_specs = (P("dp", "rot", None), P("rot", "dp", None))
    return jax.shard_map(on_device, mesh=mesh, in_specs=in_specs, out_specs=out_specs, check_vma=False)
```
